128 devices in a mesh: row: 32 (over x, y_hi, z), col: 4 (over y_lo, core).
Axes of the slice: x: 4, y: 4 (y_hi: 2, y_lo: 2; y = y_hi * 2 + y_lo), z: 4, core: 2. Of those that a mesh axis runs over, the one named last changes fastest.
Arguments:
- image: bfloat16 [1024, 512, 256], P('row', 'col'), may hold values from -6 to 6
- w_expand: bfloat16 [256, 1024], replicated, may hold values from -0.375 to 0.375
- depth_kernel: bfloat16 [3, 3, 1024], replicated, may hold values from -2 to 2
- w_project: bfloat16 [1024, 256], replicated, may hold values from -0.1875 to 0.1875
- block_qkv: bfloat16 [256, 768], replicated, may hold values from -0.375 to 0.375
- block_out: bfloat16 [256, 256], replicated, may hold values from -0.375 to 0.375
- block_bias: float32 [8, 64, 64], replicated, may hold values from -3 to 250, as said below
- grid_qkv: bfloat16 [256, 768], replicated, may hold values from -0.375 to 0.375
- grid_out: bfloat16 [256, 256], replicated, may hold values from -0.375 to 0.375
- grid_bias: float32 [8, 64, 64], replicated, may hold values from -3 to 250, as said below
Outputs:
- result: bfloat16 [1024, 512, 256], P('row', 'col')
The draws below stay inside these ranges and needn't reach their ends.
Inputs may be any that keep to these rules, and one draw needn't show every extreme that they name: `block_bias`: A learned bias for each head and each pair of query and key positions of a group. `grid_bias`: A learned bias for each head and each pair of query and key positions of a group.
All inputs are finite; a program needn't handle non-finite values.
Results may differ from the reference program's by a relative error of at most 0.012.
Values may be sent and summed in bfloat16 or wider, within the bound.
A program may use at most 128 MiB of HBM per device.

```python
import jax
import jax.numpy as jnp
from jax import lax

WIDTH = 256
HEAD_DIM = 32
WINDOW = 8
HEADS = 8
EXPANDED = 1024
ROWS_DEV = 32
NROWS = 1024
NCOLS = 512


def bias_table(key):
    span = WINDOW * WINDOW
    table = jax.random.truncated_normal(jax.random.fold_in(key, 0), -3.0, 3.0, (HEADS, span, span), jnp.float32)
    return table


def draw_block_bias(key, part):
    key = jax.random.fold_in(key, 11)
    return bias_table(key)


def draw_grid_bias(key, part):
    key = jax.random.fold_in(key, 23)
    return bias_table(key)


def shard_levels(rng, extent, shards, low, high):
    gain, own = 1.0, jax.random.fold_in(rng, 6)
    for position, shards_of in shards:
        draws = jnp.exp(jax.random.uniform(jax.random.fold_in(own, position), (shards_of,), jnp.float32, low / len(shards), high / len(shards)))
        gain = gain * jnp.repeat(draws, extent[position] // shards_of).reshape([-1 if axis == position else 1 for axis in range(len(extent))])
    return gain


def normal_values(rng, dims, deviation, limit, shards=(), kind=jnp.bfloat16):
    gain = shard_levels(rng, dims, shards, -0.22, 0.18) if shards else 1.0
    entries = jax.random.normal(rng, dims, jnp.float32) * deviation * gain
    return jnp.minimum(jnp.maximum(entries, -limit), limit).astype(kind)


def setup_inputs(seed: int = 0) -> dict:
    seeds = jax.random.split(jax.random.key(seed), 11)
    return {
        "image": normal_values(seeds[0], (NROWS, NCOLS, WIDTH), 1.0, 6.0, ((0, 32), (1, 4))),
        "w_expand": normal_values(seeds[1], (WIDTH, EXPANDED), WIDTH ** -0.5, 0.375),
        "depth_kernel": normal_values(seeds[2], (3, 3, EXPANDED), 9 ** -0.5, 2.0),
        "w_project": normal_values(seeds[3], (EXPANDED, WIDTH), EXPANDED ** -0.5, 0.1875),
        "block_qkv": normal_values(seeds[4], (WIDTH, 3 * WIDTH), WIDTH ** -0.5, 0.375),
        "block_out": normal_values(seeds[5], (WIDTH, WIDTH), WIDTH ** -0.5, 0.375),
        "block_bias": draw_block_bias(jax.random.fold_in(seeds[10], 71), 0),
        "grid_qkv": normal_values(seeds[7], (WIDTH, 3 * WIDTH), WIDTH ** -0.5, 0.375),
        "grid_out": normal_values(seeds[8], (WIDTH, WIDTH), WIDTH ** -0.5, 0.375),
        "grid_bias": draw_grid_bias(jax.random.fold_in(seeds[10], 71), 0),
    }


def layer_norm(values):
    values = values.astype(jnp.float32)
    centered = values - lax.optimization_barrier(jnp.mean(values, axis=-1, keepdims=True))
    spread = lax.optimization_barrier(jnp.mean(centered * centered, axis=-1, keepdims=True))
    return centered * lax.rsqrt(spread + 1e-05)

def expand_rows(values, w_expand):
    shape = values.shape
    normed = layer_norm(values).astype(jnp.bfloat16).reshape(-1, shape[-1])
    hidden = jax.nn.gelu(jnp.dot(normed, w_expand, preferred_element_type=jnp.float32), approximate=False)
    return hidden.astype(jnp.bfloat16).reshape(shape[:-1] + (w_expand.shape[1],))

def depthwise(padded, kernel, rows, cols):
    total = jnp.zeros((rows, cols, kernel.shape[2]), jnp.float32)
    for down in range(3):
        for across in range(3):
            total = total + padded[down:down + rows, across:across + cols].astype(jnp.float32) * kernel[down, across].astype(jnp.float32)
    return total

def attend(tokens, w_qkv, w_out, bias):
    count, span, width = tokens.shape
    heads = width // HEAD_DIM
    normed = layer_norm(tokens).astype(jnp.bfloat16).reshape(-1, width)
    packed = jnp.dot(normed, w_qkv, preferred_element_type=jnp.float32).astype(jnp.bfloat16)
    packed = packed.reshape(count, span, 3, heads, HEAD_DIM).astype(jnp.float32)
    scores = jnp.einsum('gqhd,gkhd->ghqk', packed[:, :, 0], packed[:, :, 1]) / jnp.sqrt(jnp.float32(HEAD_DIM))
    weights = jax.nn.softmax(scores + bias[None].astype(jnp.float32), axis=-1).astype(jnp.bfloat16)
    mixed = jnp.einsum('ghqk,gkhd->gqhd', weights.astype(jnp.float32), packed[:, :, 2]).astype(jnp.bfloat16)
    mixed = mixed.reshape(count * span, width)
    output = tokens.reshape(-1, width).astype(jnp.float32) + jnp.dot(mixed, w_out, preferred_element_type=jnp.float32)
    return output.astype(jnp.bfloat16).reshape(count, span, width)

def attend_all(groups, w_qkv, w_out, bias):
    total = groups.shape[0]
    block = min(256, total)
    stacked = groups.reshape(total // block, block, groups.shape[1], groups.shape[2])
    done = lax.map(lambda piece: attend(piece, w_qkv, w_out, bias), stacked)
    return done.reshape(groups.shape)

def reference(image, w_expand, depth_kernel, w_project, block_qkv, block_out, block_bias, grid_qkv, grid_out, grid_bias):
    width = image.shape[2]
    band = ROWS_DEV
    padded = jnp.pad(image, ((1, 1), (0, 0), (0, 0)))

    def conv_band(index):
        start = (index * band).astype(jnp.int32)
        rows = lax.dynamic_slice_in_dim(padded, start, band + 2, 0)
        hidden = expand_rows(rows, w_expand)
        hidden = jnp.pad(hidden, ((0, 0), (1, 1), (0, 0)))
        activated = jax.nn.gelu(depthwise(hidden, depth_kernel, band, NCOLS), approximate=False).astype(jnp.bfloat16)
        update = jnp.dot(activated.reshape(-1, activated.shape[2]), w_project, preferred_element_type=jnp.float32)
        own = lax.dynamic_slice_in_dim(image, start, band, 0).reshape(-1, width).astype(jnp.float32)
        return (own + update).astype(jnp.bfloat16).reshape(band, NCOLS, width)
    first = lax.map(conv_band, jnp.arange(NROWS // band, dtype=jnp.int32)).reshape(NROWS, NCOLS, width)
    windows = first.reshape(NROWS // WINDOW, WINDOW, NCOLS // WINDOW, WINDOW, width).transpose(0, 2, 1, 3, 4)
    windows = windows.reshape(-1, WINDOW * WINDOW, width)
    second = attend_all(windows, block_qkv, block_out, block_bias)
    second = second.reshape(NROWS // WINDOW, NCOLS // WINDOW, WINDOW, WINDOW, width).transpose(0, 2, 1, 3, 4).reshape(NROWS, NCOLS, width)
    stride_r = NROWS // WINDOW
    stride_c = NCOLS // WINDOW
    groups = second.reshape(WINDOW, stride_r, WINDOW, stride_c, width).transpose(1, 3, 0, 2, 4)
    groups = groups.reshape(-1, WINDOW * WINDOW, width)
    third = attend_all(groups, grid_qkv, grid_out, grid_bias)
    third = third.reshape(stride_r, stride_c, WINDOW, WINDOW, width).transpose(2, 0, 3, 1, 4)
    return third.reshape(NROWS, NCOLS, width)
```

```python
import functools

import jax
import jax.numpy as jnp
from jax import lax
from jax.experimental import pallas as pl
from jax.experimental.pallas import tpu as pltpu
from jax.sharding import PartitionSpec as P

MESH = pl.DeviceIdType.MESH
HEADS = 8
HEAD_DIM = 32
WIDTH = 256
EXPANDED = 1024
LOG2E = 1.4426950408889634
ROOT2 = 1.4142135623730951
BF = jnp.bfloat16
F32 = jnp.float32


def dot(a, b):
    return jnp.dot(a, b, preferred_element_type=F32)


def dot_nt(a, b):
    return lax.dot_general(a, b, (((1,), (1,)), ((), ())), preferred_element_type=F32)


def layer_norm(v):
    mean = jnp.mean(v, axis=-1, keepdims=True)
    cen = v - mean
    var = jnp.mean(cen * cen, axis=-1, keepdims=True)
    return cen * lax.rsqrt(var + 1e-5)


def gelu_of_half(z):
    return z + z * lax.erf(z * jnp.asarray(ROOT2, z.dtype))


def perm_image():
    out = lax.broadcasted_iota(jnp.int32, (256, 256), 0)
    src = lax.broadcasted_iota(jnp.int32, (256, 256), 1)
    want = (out & 128) | ((out & 15) << 3) | ((out >> 4) & 7)
    return (src == want).astype(F32).astype(BF)


def perm_image_back():
    out = lax.broadcasted_iota(jnp.int32, (256, 256), 0)
    src = lax.broadcasted_iota(jnp.int32, (256, 256), 1)
    want = (out & 128) | ((out & 7) << 4) | ((out >> 3) & 15)
    return (src == want).astype(F32).astype(BF)


def perm_swap():
    out = lax.broadcasted_iota(jnp.int32, (256, 256), 0)
    src = lax.broadcasted_iota(jnp.int32, (256, 256), 1)
    want = ((out & 15) << 4) | (out >> 4)
    return (src == want).astype(F32).astype(BF)


def perm_grid():
    out = lax.broadcasted_iota(jnp.int32, (256, 256), 0)
    src = lax.broadcasted_iota(jnp.int32, (256, 256), 1)
    group, pos = out >> 4, out & 15
    j0, s = group >> 3, group & 7
    want = ((pos >> 1) << 5) | (j0 << 4) | ((pos & 1) << 3) | s
    return (src == want).astype(F32).astype(BF)


def perm_grid_back():
    out = lax.broadcasted_iota(jnp.int32, (256, 256), 0)
    src = lax.broadcasted_iota(jnp.int32, (256, 256), 1)
    msg, j0, jl, s = out >> 5, (out >> 4) & 1, (out >> 3) & 1, out & 7
    want = (((j0 << 3) | s) << 4) | (msg << 1) | jl
    return (src == want).astype(F32).astype(BF)


def spread(x, masks, zero):
    parts = []
    for t in range(4):
        lo, hi = x[16 * t : 16 * t + 16, :128], x[16 * t : 16 * t + 16, 128:]
        for h in range(4):
            parts.append(jnp.concatenate([lo * masks[h], zero], axis=1))
        for h in range(4):
            parts.append(jnp.concatenate([zero, hi * masks[h]], axis=1))
    return jnp.concatenate(parts, axis=0)


def attention(tok, res, w_qkv, w_out, bias, ones):
    lane = lax.broadcasted_iota(jnp.int32, (64, 128), 1)
    mlane = lax.broadcasted_iota(jnp.int32, (16, 128), 1)
    masks = [(mlane // HEAD_DIM == h).astype(F32).astype(BF) for h in range(4)]
    zero = jnp.zeros((16, 128), BF)

    def step(c, carry):
        t = tok[pl.ds(4 * c, 4)].reshape(256, WIDTH)
        normed = layer_norm(t).astype(BF)
        qkv = dot(normed, w_qkv[...])
        q = (qkv[:, :WIDTH] * (LOG2E / HEAD_DIM**0.5)).astype(BF)
        k = qkv[:, WIDTH : 2 * WIDTH].astype(BF)
        v = qkv[:, 2 * WIDTH :].astype(BF)
        mixed = []
        for g in range(4):
            rows = slice(64 * g, 64 * g + 64)
            z = dot_nt(q[rows], spread(k[rows], masks, zero)) + bias[...]
            tiles = [z[:, 128 * n : 128 * n + 128] for n in range(4)]
            m = jnp.maximum(jnp.maximum(tiles[0], tiles[1]), jnp.maximum(tiles[2], tiles[3]))
            for bit in (8, 4, 2, 1):
                m = jnp.maximum(m, jnp.take_along_axis(m, lane ^ bit, axis=1))
            p = jnp.concatenate([jnp.exp2(x - m).astype(BF) for x in tiles], axis=1)
            num = dot(p, spread(v[rows], masks, zero))
            den = dot(p, ones[...])
            mixed.append((num / den).astype(BF))
        out = dot(jnp.concatenate(mixed, axis=0), w_out[...]) + t
        res[pl.ds(4 * c, 4)] = out.astype(BF).reshape(4, 64, WIDTH)
        return carry

    lax.fori_loop(0, 4, step, 0)


def kernel(
    image, w_expand, depth, w_project, b_qkv, b_out, b_bias, g_qkv, g_out, g_bias,
    result,
    halo_tb, halo_l, halo_r, edge_l, edge_r, send1, recv1, send2, recv2,
    hidden, image_p, w_half, taps, hid_l, hid_r, act, tok, res, perms, ones,
    halo_send, halo_recv, send_sem1, recv_sem1, send_sem2, recv_sem2,
):
    R, C = lax.axis_index("row"), lax.axis_index("col")
    plane, mine = R % 4, (R // 4) * 4 + C

    def device(d):
        return {"row": (d // 4) * 4 + plane, "col": d % 4}

    up, down = (R + 31) % 32, (R + 1) % 32
    left, right = (C + 3) % 4, (C + 1) % 4

    barrier = pltpu.get_barrier_semaphore()

    def greet(n, carry):
        pl.semaphore_signal(barrier, inc=1, device_id=device((mine + n) % 32), device_id_type=MESH)
        return carry

    lax.fori_loop(1, 32, greet, 0)
    for r in (up, down):
        for c in (left, C, right):
            pl.semaphore_signal(barrier, inc=1, device_id={"row": r, "col": c}, device_id_type=MESH)

    perms[0] = perm_image()
    perms[1] = perm_image_back()
    perms[2] = perm_swap()
    perms[3] = perm_grid()
    perms[4] = perm_grid_back()
    row_head = (lax.broadcasted_iota(jnp.int32, (512, WIDTH), 0) // 16) % HEADS
    lane_head = lax.broadcasted_iota(jnp.int32, (512, WIDTH), 1) // HEAD_DIM
    ones[...] = (row_head == lane_head).astype(F32).astype(BF)
    w_half[...] = w_expand[...] * jnp.asarray(0.5, BF)
    for n in range(9):
        tap = depth[n // 3, pl.ds(n % 3, 1), :].astype(F32) * 0.5
        taps[n] = jnp.broadcast_to(tap, (16, EXPANDED)).astype(BF)
    row16 = lax.broadcasted_iota(jnp.int32, (32, 16, WIDTH), 1)
    edge_l[...] = jnp.sum(
        jnp.where(row16 == 0, image[:, 0:16, :].astype(F32), 0.0), axis=1
    ).astype(BF)
    edge_r[...] = jnp.sum(
        jnp.where(row16 == 15, image[:, 112:128, :].astype(F32), 0.0), axis=1
    ).astype(BF)

    def expand(tokens, row0, row1, keep):
        x = dot(perms[0], tokens)
        if keep is not None:
            image_p[keep] = x.astype(BF)
        normed = layer_norm(x).astype(BF)
        for n in range(4):
            ch = slice(256 * n, 256 * n + 256)
            h = gelu_of_half(dot(normed, w_half[:, ch])).astype(BF)
            hidden[row0, 1:9, :, ch] = h[:128].reshape(8, 16, 256)
            hidden[row1, 1:9, :, ch] = h[128:].reshape(8, 16, 256)

    def expand_image(b):
        rows = image[pl.ds(2 * b, 2)].reshape(256, WIDTH)
        expand(rows, 2 * b + 1, 2 * b + 2, b)

    expand_image(0)
    pl.semaphore_wait(barrier, 37)

    def halo_copies():
        plan = (
            (image.at[31], halo_tb.at[0], down, C),
            (image.at[0], halo_tb.at[1], up, C),
            (edge_r, halo_l.at[pl.ds(16, 32)], R, right),
            (edge_l, halo_r.at[pl.ds(16, 32)], R, left),
            (edge_r.at[pl.ds(16, 16)], halo_l.at[pl.ds(0, 16)], down, right),
            (edge_r.at[pl.ds(0, 16)], halo_l.at[pl.ds(48, 16)], up, right),
            (edge_l.at[pl.ds(16, 16)], halo_r.at[pl.ds(0, 16)], down, left),
            (edge_l.at[pl.ds(0, 16)], halo_r.at[pl.ds(48, 16)], up, left),
        )
        return [
            pltpu.make_async_remote_copy(
                src_ref=src, dst_ref=dst, send_sem=halo_send.at[n], recv_sem=halo_recv.at[n],
                device_id={"row": r, "col": c}, device_id_type=MESH,
            )
            for n, (src, dst, r, c) in enumerate(plan)
        ]

    halos = halo_copies()
    for copy in halos:
        copy.start()
    expand_image(1)
    for copy in halos:
        copy.wait()

    row64 = lax.broadcasted_iota(jnp.int32, (64, WIDTH), 0)
    off_grid = ((row64 <= 15) & (R == 0)) | ((row64 >= 48) & (R == 31))
    for halo, off, hid in ((halo_l, C == 0, hid_l), (halo_r, C == 3, hid_r)):
        x = jnp.where(off_grid | off, 0.0, halo[...].astype(F32))
        hid[...] = gelu_of_half(dot(layer_norm(x).astype(BF), w_half[...]))
    row256 = lax.broadcasted_iota(jnp.int32, (256, WIDTH), 0)
    off_grid = ((row256 < 128) & (R == 0)) | ((row256 >= 128) & (R == 31))
    x = jnp.where(off_grid, 0.0, halo_tb[...].reshape(256, WIDTH).astype(F32)).astype(BF)
    expand(x, 0, 33, None)

    row_s = lax.broadcasted_iota(jnp.int32, (16, EXPANDED), 0)

    def edges(r):
        from_left = pltpu.roll(hidden[r, 8].astype(F32), 1, 0)
        hidden[r, 0] = jnp.where(row_s == 0, hid_l[pl.ds(15 + r, 1), :], from_left).astype(BF)
        from_right = pltpu.roll(hidden[r, 1].astype(F32), 15, 0)
        hidden[r, 9] = jnp.where(row_s == 15, hid_r[pl.ds(15 + r, 1), :], from_right).astype(BF)

    for r in range(2):
        edges(r)

    def convolve(b):
        for row in range(2):
            for n in range(8):
                ch = slice(128 * n, 128 * n + 128)
                total = None
                for dr in range(3):
                    for dc in range(3):
                        term = hidden[2 * b + row + dr, dc : dc + 8, :, ch] * taps[3 * dr + dc, :, ch]
                        total = term if total is None else total + term
                act[128 * row : 128 * row + 128, ch] = gelu_of_half(total).reshape(128, 128)
        update = dot(act[...], w_project[...])
        return (image_p[b].astype(F32) + update).astype(BF)

    def exchange(src_of, dst_of, send_sem, recv_sem):
        own = pltpu.make_async_copy(src_of(mine), dst_of(mine), recv_sem)
        own.start()

        def send(n, carry):
            d = (mine + n) % 32
            pltpu.make_async_remote_copy(
                src_ref=src_of(d), dst_ref=dst_of(mine), send_sem=send_sem, recv_sem=recv_sem,
                device_id=device(d), device_id_type=MESH,
            ).start()
            return carry

        lax.fori_loop(1, 32, send, 0)

    def image_part(buf, k):
        return lambda d: buf.at[8 * k + d // 4, pl.ds(2 * (d % 4), 2)]

    def grid_part(buf, k):
        return lambda d: buf.at[k, d]

    def reorder_out(perm, store):
        for n in range(4):
            block = res[:, 16 * n : 16 * n + 16, :].reshape(256, WIDTH)
            store(n, dot(perm, block).astype(BF))

    def band(k, carry):
        @pl.when(k < 4)
        def _():
            def rows(n, carry):
                b = 4 * k + n

                @pl.when(b < 14)
                def _():
                    expand_image(b + 2)

                edges(2 * b + 2)
                edges(2 * b + 3)
                first = convolve(b)
                swapped = dot(perms[2], first).reshape(16, 16, WIDTH)
                tok[:, pl.ds(pl.multiple_of(16 * n, 16), 16), :] = swapped
                return carry

            lax.fori_loop(0, 4, rows, 0)
            attention(tok, res, b_qkv, b_out, b_bias, ones)

            def store(n, x):
                send1[pl.ds(8 * k + 2 * n, 2)] = x.reshape(2, 8, 16, WIDTH)

            reorder_out(perms[2], store)
            exchange(image_part(send1, k), grid_part(recv1, k), send_sem1.at[k], recv_sem1.at[k])

        @pl.when(k >= 1)
        def _():
            g = k - 1
            pltpu.make_async_copy(recv1.at[g], recv1.at[g], recv_sem1.at[g]).wait()
            for n in range(4):
                x = recv1[g, 8 * n : 8 * n + 8].reshape(256, WIDTH)
                tok[:, 16 * n : 16 * n + 16, :] = dot(perms[3], x).reshape(16, 16, WIDTH)
            attention(tok, res, g_qkv, g_out, g_bias, ones)

            def store(n, x):
                send2[g, 8 * n : 8 * n + 8] = x.reshape(8, 2, 16, WIDTH)

            reorder_out(perms[4], store)
            exchange_back(g)

        return carry

    def exchange_back(g):
        own = pltpu.make_async_copy(send2.at[g, mine], image_part(recv2, g)(mine), recv_sem2.at[g])
        own.start()

        def send(n, carry):
            d = (mine + n) % 32
            pltpu.make_async_remote_copy(
                src_ref=send2.at[g, d], dst_ref=image_part(recv2, g)(mine),
                send_sem=send_sem2.at[g], recv_sem=recv_sem2.at[g],
                device_id=device(d), device_id_type=MESH,
            ).start()
            return carry

        lax.fori_loop(1, 32, send, 0)

    lax.fori_loop(0, 5, band, 0)

    def finish(g, carry):
        view = recv2.at[pl.ds(8 * g, 8)]
        pltpu.make_async_copy(view, view, recv_sem2.at[g]).wait()
        for n in range(4):
            x = recv2[pl.ds(8 * g + 2 * n, 2)].reshape(256, WIDTH)
            result[pl.ds(8 * g + 2 * n, 2)] = dot(perms[1], x).astype(BF).reshape(2, 128, WIDTH)
        return carry

    lax.fori_loop(0, 4, finish, 0)

    def drain(g, carry):
        part = send2.at[g, pl.ds(0, 31)]
        pltpu.make_async_copy(part, part, send_sem1.at[g]).wait()
        pltpu.make_async_copy(part, part, send_sem2.at[g]).wait()
        return carry

    lax.fori_loop(0, 4, drain, 0)


def in_tiles(bias):
    tiled = (bias * LOG2E).reshape(HEADS, 64, 4, 16).transpose(1, 2, 0, 3)
    return tiled.reshape(64, 512)


def on_device(image, w_expand, depth, w_project, b_qkv, b_out, b_bias, g_qkv, g_out, g_bias):
    vmem = pl.BlockSpec(memory_space=pltpu.VMEM)
    dma = pltpu.SemaphoreType.DMA
    return pl.pallas_call(
        kernel,
        out_shape=jax.ShapeDtypeStruct(image.shape, BF),
        in_specs=[vmem] * 10,
        out_specs=vmem,
        scratch_shapes=[
            pltpu.VMEM((2, 128, WIDTH), BF),
            pltpu.VMEM((64, WIDTH), BF),
            pltpu.VMEM((64, WIDTH), BF),
            pltpu.VMEM((32, WIDTH), BF),
            pltpu.VMEM((32, WIDTH), BF),
            pltpu.VMEM((32, 8, 16, WIDTH), BF),
            pltpu.VMEM((4, 32, 2, 16, WIDTH), BF),
            pltpu.VMEM((4, 32, 2, 16, WIDTH), BF),
            pltpu.VMEM((32, 8, 16, WIDTH), BF),
            pltpu.VMEM((34, 10, 16, EXPANDED), BF),
            pltpu.VMEM((16, 256, WIDTH), BF),
            pltpu.VMEM((WIDTH, EXPANDED), BF),
            pltpu.VMEM((9, 16, EXPANDED), BF),
            pltpu.VMEM((64, EXPANDED), F32),
            pltpu.VMEM((64, EXPANDED), F32),
            pltpu.VMEM((256, EXPANDED), BF),
            pltpu.VMEM((16, 64, WIDTH), F32),
            pltpu.VMEM((16, 64, WIDTH), BF),
            pltpu.VMEM((5, 256, 256), BF),
            pltpu.VMEM((512, WIDTH), BF),
            dma((8,)),
            dma((8,)),
            dma((4,)),
            dma((4,)),
            dma((4,)),
            dma((4,)),
        ],
        compiler_params=pltpu.CompilerParams(
            collective_id=0, has_side_effects=True, vmem_limit_bytes=56 << 20
        ),
    )(
        image, w_expand, depth, w_project, b_qkv, b_out, in_tiles(b_bias),
        g_qkv, g_out, in_tiles(g_bias),
    )


def solution(mesh):
    in_specs = (P("row", "col", None),) + (P(),) * 9
    return jax.shard_map(
        on_device, mesh=mesh, in_specs=in_specs, out_specs=P("row", "col", None), check_vma=False
    )
```

```python
import functools

import jax
import jax.numpy as jnp
from jax import lax
from jax.experimental import pallas as pl
from jax.experimental.pallas import tpu as pltpu
from jax.sharding import PartitionSpec as P

MESH = pl.DeviceIdType.MESH
HEADS = 8
HEAD_DIM = 32
WIDTH = 256
EXPANDED = 1024
LOG2E = 1.4426950408889634
ROOT2 = 1.4142135623730951
BF = jnp.bfloat16
F32 = jnp.float32


def dot(a, b):
    return jnp.dot(a, b, preferred_element_type=F32)


def dot_nt(a, b):
    return lax.dot_general(a, b, (((1,), (1,)), ((), ())), preferred_element_type=F32)


def layer_norm(v):
    mean = jnp.mean(v, axis=-1, keepdims=True)
    cen = v - mean
    var = jnp.mean(cen * cen, axis=-1, keepdims=True)
    return cen * lax.rsqrt(var + 1e-5)


def gelu_of_half(z):
    return z + z * lax.erf(z * jnp.asarray(ROOT2, z.dtype))


def perm_image():
    out = lax.broadcasted_iota(jnp.int32, (256, 256), 0)
    src = lax.broadcasted_iota(jnp.int32, (256, 256), 1)
    want = (out & 128) | ((out & 15) << 3) | ((out >> 4) & 7)
    return (src == want).astype(F32).astype(BF)


def perm_image_back():
    out = lax.broadcasted_iota(jnp.int32, (256, 256), 0)
    src = lax.broadcasted_iota(jnp.int32, (256, 256), 1)
    want = (out & 128) | ((out & 7) << 4) | ((out >> 3) & 15)
    return (src == want).astype(F32).astype(BF)


def perm_swap():
    out = lax.broadcasted_iota(jnp.int32, (256, 256), 0)
    src = lax.broadcasted_iota(jnp.int32, (256, 256), 1)
    want = ((out & 15) << 4) | (out >> 4)
    return (src == want).astype(F32).astype(BF)


def perm_grid():
    out = lax.broadcasted_iota(jnp.int32, (256, 256), 0)
    src = lax.broadcasted_iota(jnp.int32, (256, 256), 1)
    group, pos = out >> 4, out & 15
    j0, s = group >> 3, group & 7
    want = ((pos >> 1) << 5) | (j0 << 4) | ((pos & 1) << 3) | s
    return (src == want).astype(F32).astype(BF)


def perm_grid_back():
    out = lax.broadcasted_iota(jnp.int32, (256, 256), 0)
    src = lax.broadcasted_iota(jnp.int32, (256, 256), 1)
    msg, j0, jl, s = out >> 5, (out >> 4) & 1, (out >> 3) & 1, out & 7
    want = (((j0 << 3) | s) << 4) | (msg << 1) | jl
    return (src == want).astype(F32).astype(BF)


def spread(x, masks, zero):
    parts = []
    for t in range(4):
        lo, hi = x[16 * t : 16 * t + 16, :128], x[16 * t : 16 * t + 16, 128:]
        for h in range(4):
            parts.append(jnp.concatenate([lo * masks[h], zero], axis=1))
        for h in range(4):
            parts.append(jnp.concatenate([zero, hi * masks[h]], axis=1))
    return jnp.concatenate(parts, axis=0)


def attention(tok, res, w_qkv, w_out, bias, ones):
    lane = lax.broadcasted_iota(jnp.int32, (256, 128), 1)
    mlane = lax.broadcasted_iota(jnp.int32, (16, 128), 1)
    masks = [(mlane // HEAD_DIM == h).astype(F32).astype(BF) for h in range(4)]
    zero = jnp.zeros((16, 128), BF)

    def step(c, carry):
        t = tok[pl.ds(4 * c, 4)].reshape(256, WIDTH)
        normed = layer_norm(t).astype(BF)
        qkv = dot(normed, w_qkv[...])
        q = (qkv[:, :WIDTH] * (LOG2E / HEAD_DIM**0.5)).astype(BF)
        k = qkv[:, WIDTH : 2 * WIDTH].astype(BF)
        v = qkv[:, 2 * WIDTH :].astype(BF)
        groups = [slice(64 * g, 64 * g + 64) for g in range(4)]
        scores = [dot_nt(q[rows], spread(k[rows], masks, zero)) + bias[...] for rows in groups]
        z = jnp.concatenate(scores, axis=0)
        tiles = [z[:, 128 * n : 128 * n + 128] for n in range(4)]
        m = jnp.maximum(jnp.maximum(tiles[0], tiles[1]), jnp.maximum(tiles[2], tiles[3]))
        for bit in (8, 4, 2, 1):
            m = jnp.maximum(m, jnp.take_along_axis(m, lane ^ bit, axis=1))
        p = jnp.concatenate([jnp.exp2(x - m).astype(BF) for x in tiles], axis=1)
        den = dot(p, ones[...])
        num = jnp.concatenate([dot(p[rows], spread(v[rows], masks, zero)) for rows in groups], axis=0)
        mixed = (num / den).astype(BF)
        out = dot(mixed, w_out[...]) + t
        res[pl.ds(4 * c, 4)] = out.astype(BF).reshape(4, 64, WIDTH)
        return carry

    lax.fori_loop(0, 4, step, 0)


def kernel(
    image, w_expand, depth, w_project, b_qkv, b_out, b_bias, g_qkv, g_out, g_bias,
    result,
    halo_tb, halo_l, halo_r, edge_l, edge_r, send1, recv1, send2, recv2,
    hidden, image_p, w_half, taps, hid_l, hid_r, act, tok, res, perms, ones,
    halo_send, halo_recv, send_sem1, recv_sem1, send_sem2, recv_sem2,
):
    R, C = lax.axis_index("row"), lax.axis_index("col")
    plane, mine = R % 4, (R // 4) * 4 + C

    def device(d):
        return {"row": (d // 4) * 4 + plane, "col": d % 4}

    up, down = (R + 31) % 32, (R + 1) % 32
    left, right = (C + 3) % 4, (C + 1) % 4

    barrier = pltpu.get_barrier_semaphore()

    def greet(n, carry):
        pl.semaphore_signal(barrier, inc=1, device_id=device((mine + n) % 32), device_id_type=MESH)
        return carry

    lax.fori_loop(1, 32, greet, 0)
    for r in (up, down):
        for c in (left, C, right):
            pl.semaphore_signal(barrier, inc=1, device_id={"row": r, "col": c}, device_id_type=MESH)

    perms[0] = perm_image()
    perms[1] = perm_image_back()
    perms[2] = perm_swap()
    perms[3] = perm_grid()
    perms[4] = perm_grid_back()
    row_head = (lax.broadcasted_iota(jnp.int32, (512, WIDTH), 0) // 16) % HEADS
    lane_head = lax.broadcasted_iota(jnp.int32, (512, WIDTH), 1) // HEAD_DIM
    ones[...] = (row_head == lane_head).astype(F32).astype(BF)
    w_half[...] = w_expand[...] * jnp.asarray(0.5, BF)
    for n in range(9):
        tap = depth[n // 3, pl.ds(n % 3, 1), :].astype(F32) * 0.5
        taps[n] = jnp.broadcast_to(tap, (16, EXPANDED)).astype(BF)
    row16 = lax.broadcasted_iota(jnp.int32, (32, 16, WIDTH), 1)
    edge_l[...] = jnp.sum(
        jnp.where(row16 == 0, image[:, 0:16, :].astype(F32), 0.0), axis=1
    ).astype(BF)
    edge_r[...] = jnp.sum(
        jnp.where(row16 == 15, image[:, 112:128, :].astype(F32), 0.0), axis=1
    ).astype(BF)

    def expand(tokens, row0, row1, keep):
        x = dot(perms[0], tokens)
        if keep is not None:
            image_p[keep] = x.astype(BF)
        normed = layer_norm(x).astype(BF)
        for n in range(4):
            ch = slice(256 * n, 256 * n + 256)
            h = gelu_of_half(dot(normed, w_half[:, ch])).astype(BF)
            hidden[row0, 1:9, :, ch] = h[:128].reshape(8, 16, 256)
            hidden[row1, 1:9, :, ch] = h[128:].reshape(8, 16, 256)

    def expand_image(b):
        rows = image[pl.ds(2 * b, 2)].reshape(256, WIDTH)
        expand(rows, 2 * b + 1, 2 * b + 2, b)

    expand_image(0)
    pl.semaphore_wait(barrier, 37)

    def halo_copies():
        plan = (
            (image.at[31], halo_tb.at[0], down, C),
            (image.at[0], halo_tb.at[1], up, C),
            (edge_r, halo_l.at[pl.ds(16, 32)], R, right),
            (edge_l, halo_r.at[pl.ds(16, 32)], R, left),
            (edge_r.at[pl.ds(16, 16)], halo_l.at[pl.ds(0, 16)], down, right),
            (edge_r.at[pl.ds(0, 16)], halo_l.at[pl.ds(48, 16)], up, right),
            (edge_l.at[pl.ds(16, 16)], halo_r.at[pl.ds(0, 16)], down, left),
            (edge_l.at[pl.ds(0, 16)], halo_r.at[pl.ds(48, 16)], up, left),
        )
        return [
            pltpu.make_async_remote_copy(
                src_ref=src, dst_ref=dst, send_sem=halo_send.at[n], recv_sem=halo_recv.at[n],
                device_id={"row": r, "col": c}, device_id_type=MESH,
            )
            for n, (src, dst, r, c) in enumerate(plan)
        ]

    halos = halo_copies()
    for copy in halos:
        copy.start()
    expand_image(1)
    for copy in halos:
        copy.wait()

    row64 = lax.broadcasted_iota(jnp.int32, (64, WIDTH), 0)
    off_grid = ((row64 <= 15) & (R == 0)) | ((row64 >= 48) & (R == 31))
    for halo, off, hid in ((halo_l, C == 0, hid_l), (halo_r, C == 3, hid_r)):
        x = jnp.where(off_grid | off, 0.0, halo[...].astype(F32))
        hid[...] = gelu_of_half(dot(layer_norm(x).astype(BF), w_half[...]))
    row256 = lax.broadcasted_iota(jnp.int32, (256, WIDTH), 0)
    off_grid = ((row256 < 128) & (R == 0)) | ((row256 >= 128) & (R == 31))
    x = jnp.where(off_grid, 0.0, halo_tb[...].reshape(256, WIDTH).astype(F32)).astype(BF)
    expand(x, 0, 33, None)

    row_s = lax.broadcasted_iota(jnp.int32, (16, EXPANDED), 0)

    def edges(r):
        from_left = pltpu.roll(hidden[r, 8].astype(F32), 1, 0)
        hidden[r, 0] = jnp.where(row_s == 0, hid_l[pl.ds(15 + r, 1), :], from_left).astype(BF)
        from_right = pltpu.roll(hidden[r, 1].astype(F32), 15, 0)
        hidden[r, 9] = jnp.where(row_s == 15, hid_r[pl.ds(15 + r, 1), :], from_right).astype(BF)

    for r in range(2):
        edges(r)

    def convolve(b):
        for row in range(2):
            for n in range(8):
                ch = slice(128 * n, 128 * n + 128)
                total = None
                for dr in range(3):
                    for dc in range(3):
                        term = hidden[2 * b + row + dr, dc : dc + 8, :, ch] * taps[3 * dr + dc, :, ch]
                        total = term if total is None else total + term
                act[128 * row : 128 * row + 128, ch] = gelu_of_half(total).reshape(128, 128)
        update = dot(act[...], w_project[...])
        return (image_p[b].astype(F32) + update).astype(BF)

    def exchange(src_of, dst_of, send_sem, recv_sem):
        own = pltpu.make_async_copy(src_of(mine), dst_of(mine), recv_sem)
        own.start()

        def send(n, carry):
            d = (mine + n) % 32
            pltpu.make_async_remote_copy(
                src_ref=src_of(d), dst_ref=dst_of(mine), send_sem=send_sem, recv_sem=recv_sem,
                device_id=device(d), device_id_type=MESH,
            ).start()
            return carry

        lax.fori_loop(1, 32, send, 0)

    def image_part(buf, k):
        return lambda d: buf.at[8 * k + d // 4, pl.ds(2 * (d % 4), 2)]

    def grid_part(buf, k):
        return lambda d: buf.at[k, d]

    def reorder_out(perm, store):
        for n in range(4):
            block = res[:, 16 * n : 16 * n + 16, :].reshape(256, WIDTH)
            store(n, dot(perm, block).astype(BF))

    def band(k, carry):
        @pl.when(k < 4)
        def _():
            def rows(n, carry):
                b = 4 * k + n

                @pl.when(b < 14)
                def _():
                    expand_image(b + 2)

                edges(2 * b + 2)
                edges(2 * b + 3)
                first = convolve(b)
                swapped = dot(perms[2], first).reshape(16, 16, WIDTH)
                tok[:, pl.ds(pl.multiple_of(16 * n, 16), 16), :] = swapped
                return carry

            lax.fori_loop(0, 4, rows, 0)
            attention(tok, res, b_qkv, b_out, b_bias, ones)

            def store(n, x):
                send1[pl.ds(8 * k + 2 * n, 2)] = x.reshape(2, 8, 16, WIDTH)

            reorder_out(perms[2], store)
            exchange(image_part(send1, k), grid_part(recv1, k), send_sem1.at[k], recv_sem1.at[k])

        @pl.when(k >= 1)
        def _():
            g = k - 1
            pltpu.make_async_copy(recv1.at[g], recv1.at[g], recv_sem1.at[g]).wait()
            for n in range(4):
                x = recv1[g, 8 * n : 8 * n + 8].reshape(256, WIDTH)
                tok[:, 16 * n : 16 * n + 16, :] = dot(perms[3], x).reshape(16, 16, WIDTH)
            attention(tok, res, g_qkv, g_out, g_bias, ones)

            def store(n, x):
                send2[g, 8 * n : 8 * n + 8] = x.reshape(8, 2, 16, WIDTH)

            reorder_out(perms[4], store)
            exchange_back(g)

        return carry

    def exchange_back(g):
        own = pltpu.make_async_copy(send2.at[g, mine], image_part(recv2, g)(mine), recv_sem2.at[g])
        own.start()

        def send(n, carry):
            d = (mine + n) % 32
            pltpu.make_async_remote_copy(
                src_ref=send2.at[g, d], dst_ref=image_part(recv2, g)(mine),
                send_sem=send_sem2.at[g], recv_sem=recv_sem2.at[g],
                device_id=device(d), device_id_type=MESH,
            ).start()
            return carry

        lax.fori_loop(1, 32, send, 0)

    lax.fori_loop(0, 5, band, 0)

    def finish(g, carry):
        view = recv2.at[pl.ds(8 * g, 8)]
        pltpu.make_async_copy(view, view, recv_sem2.at[g]).wait()
        for n in range(4):
            x = recv2[pl.ds(8 * g + 2 * n, 2)].reshape(256, WIDTH)
            result[pl.ds(8 * g + 2 * n, 2)] = dot(perms[1], x).astype(BF).reshape(2, 128, WIDTH)
        return carry

    lax.fori_loop(0, 4, finish, 0)

    def drain(g, carry):
        part = send2.at[g, pl.ds(0, 31)]
        pltpu.make_async_copy(part, part, send_sem1.at[g]).wait()
        pltpu.make_async_copy(part, part, send_sem2.at[g]).wait()
        return carry

    lax.fori_loop(0, 4, drain, 0)


def in_tiles(bias):
    tiled = (bias * LOG2E).reshape(HEADS, 64, 4, 16).transpose(1, 2, 0, 3)
    return tiled.reshape(64, 512)


def on_device(image, w_expand, depth, w_project, b_qkv, b_out, b_bias, g_qkv, g_out, g_bias):
    vmem = pl.BlockSpec(memory_space=pltpu.VMEM)
    dma = pltpu.SemaphoreType.DMA
    return pl.pallas_call(
        kernel,
        out_shape=jax.ShapeDtypeStruct(image.shape, BF),
        in_specs=[vmem] * 10,
        out_specs=vmem,
        scratch_shapes=[
            pltpu.VMEM((2, 128, WIDTH), BF),
            pltpu.VMEM((64, WIDTH), BF),
            pltpu.VMEM((64, WIDTH), BF),
            pltpu.VMEM((32, WIDTH), BF),
            pltpu.VMEM((32, WIDTH), BF),
            pltpu.VMEM((32, 8, 16, WIDTH), BF),
            pltpu.VMEM((4, 32, 2, 16, WIDTH), BF),
            pltpu.VMEM((4, 32, 2, 16, WIDTH), BF),
            pltpu.VMEM((32, 8, 16, WIDTH), BF),
            pltpu.VMEM((34, 10, 16, EXPANDED), BF),
            pltpu.VMEM((16, 256, WIDTH), BF),
            pltpu.VMEM((WIDTH, EXPANDED), BF),
            pltpu.VMEM((9, 16, EXPANDED), BF),
            pltpu.VMEM((64, EXPANDED), F32),
            pltpu.VMEM((64, EXPANDED), F32),
            pltpu.VMEM((256, EXPANDED), BF),
            pltpu.VMEM((16, 64, WIDTH), F32),
            pltpu.VMEM((16, 64, WIDTH), BF),
            pltpu.VMEM((5, 256, 256), BF),
            pltpu.VMEM((512, WIDTH), BF),
            dma((8,)),
            dma((8,)),
            dma((4,)),
            dma((4,)),
            dma((4,)),
            dma((4,)),
        ],
        compiler_params=pltpu.CompilerParams(
            collective_id=0, has_side_effects=True, vmem_limit_bytes=56 << 20
        ),
    )(
        image, w_expand, depth, w_project, b_qkv, b_out, in_tiles(b_bias),
        g_qkv, g_out, in_tiles(g_bias),
    )


def solution(mesh):
    in_specs = (P("row", "col", None),) + (P(),) * 9
    return jax.shard_map(
        on_device, mesh=mesh, in_specs=in_specs, out_specs=P("row", "col", None), check_vma=False
    )
```

```python
import functools

import jax
import jax.numpy as jnp
from jax import lax
from jax.experimental import pallas as pl
from jax.experimental.pallas import tpu as pltpu
from jax.sharding import PartitionSpec as P

MESH = pl.DeviceIdType.MESH
HEADS = 8
HEAD_DIM = 32
WIDTH = 256
EXPANDED = 1024
LOG2E = 1.4426950408889634
ROOT2 = 1.4142135623730951
BF = jnp.bfloat16
F32 = jnp.float32


def dot(a, b):
    return jnp.dot(a, b, preferred_element_type=F32)


def dot_nt(a, b):
    return lax.dot_general(a, b, (((1,), (1,)), ((), ())), preferred_element_type=F32)


def layer_norm(v):
    mean = jnp.mean(v, axis=-1, keepdims=True)
    cen = v - mean
    var = jnp.mean(cen * cen, axis=-1, keepdims=True)
    return cen * lax.rsqrt(var + 1e-5)


def gelu_of_half(z):
    return z + z * lax.erf(z * jnp.asarray(ROOT2, z.dtype))


def perm_image():
    out = lax.broadcasted_iota(jnp.int32, (256, 256), 0)
    src = lax.broadcasted_iota(jnp.int32, (256, 256), 1)
    want = (out & 128) | ((out & 15) << 3) | ((out >> 4) & 7)
    return (src == want).astype(F32).astype(BF)


def perm_image_back():
    out = lax.broadcasted_iota(jnp.int32, (256, 256), 0)
    src = lax.broadcasted_iota(jnp.int32, (256, 256), 1)
    want = (out & 128) | ((out & 7) << 4) | ((out >> 3) & 15)
    return (src == want).astype(F32).astype(BF)


def perm_swap():
    out = lax.broadcasted_iota(jnp.int32, (256, 256), 0)
    src = lax.broadcasted_iota(jnp.int32, (256, 256), 1)
    want = ((out & 15) << 4) | (out >> 4)
    return (src == want).astype(F32).astype(BF)


def perm_grid():
    out = lax.broadcasted_iota(jnp.int32, (256, 256), 0)
    src = lax.broadcasted_iota(jnp.int32, (256, 256), 1)
    group, pos = out >> 4, out & 15
    j0, s = group >> 3, group & 7
    want = ((pos >> 1) << 5) | (j0 << 4) | ((pos & 1) << 3) | s
    return (src == want).astype(F32).astype(BF)


def perm_grid_back():
    out = lax.broadcasted_iota(jnp.int32, (256, 256), 0)
    src = lax.broadcasted_iota(jnp.int32, (256, 256), 1)
    msg, j0, jl, s = out >> 5, (out >> 4) & 1, (out >> 3) & 1, out & 7
    want = (((j0 << 3) | s) << 4) | (msg << 1) | jl
    return (src == want).astype(F32).astype(BF)


def spread(x, masks):
    return jnp.concatenate(
        [x[16 * t : 16 * t + 16] * masks[h] for t in range(4) for h in range(4)], axis=0
    )


def attention(tok, res, w_qkv, w_out, bias, ones):
    lane = lax.broadcasted_iota(jnp.int32, (256, 128), 1)
    high = lane >= 64
    mlane = lax.broadcasted_iota(jnp.int32, (16, 128), 1)
    masks = [(mlane // HEAD_DIM == h).astype(F32).astype(BF) for h in range(4)]
    groups = [slice(64 * g, 64 * g + 64) for g in range(4)]
    halves = (slice(0, 128), slice(128, 256))

    def step(c, carry):
        t = tok[pl.ds(4 * c, 4)].reshape(256, WIDTH)
        normed = layer_norm(t).astype(BF)
        qkv = dot(normed, w_qkv[...])
        q = (qkv[:, :WIDTH] * (LOG2E / HEAD_DIM**0.5)).astype(BF)
        k = qkv[:, WIDTH : 2 * WIDTH].astype(BF)
        v = qkv[:, 2 * WIDTH :].astype(BF)
        tiles, tops = [], []
        for n, half in enumerate(halves):
            z = jnp.concatenate(
                [dot_nt(q[g, half], spread(k[g, half], masks)) + bias[n] for g in groups], axis=0
            )
            tiles.append((z[:, :128], z[:, 128:]))
            tops.append(jnp.maximum(z[:, :128], z[:, 128:]))
        m = jnp.maximum(
            jnp.where(high, tops[0], tops[1]), pltpu.roll(jnp.where(high, tops[1], tops[0]), 64, 1)
        )
        for bit in (8, 4, 2, 1):
            m = jnp.maximum(m, jnp.take_along_axis(m, lane ^ bit, axis=1))
        other = pltpu.roll(m, 64, 1)
        tops = (jnp.where(high, m, other), jnp.where(high, other, m))
        mixed = []
        for n, half in enumerate(halves):
            p = jnp.concatenate([jnp.exp2(x - tops[n]).astype(BF) for x in tiles[n]], axis=1)
            den = dot(p, ones[...])
            num = jnp.concatenate([dot(p[g], spread(v[g, half], masks)) for g in groups], axis=0)
            mixed.append((num / den).astype(BF))
        out = dot(jnp.concatenate(mixed, axis=1), w_out[...]) + t
        res[pl.ds(4 * c, 4)] = out.astype(BF).reshape(4, 64, WIDTH)
        return carry

    lax.fori_loop(0, 4, step, 0, unroll=4)


def kernel(
    image, w_expand, depth, w_project, b_qkv, b_out, b_bias, g_qkv, g_out, g_bias,
    result,
    halo_tb, halo_l, halo_r, edge_l, edge_r, send1, recv1, send2, recv2,
    hidden, image_p, w_half, taps, hid_l, hid_r, act, tok, res, perms, ones,
    halo_send, halo_recv, send_sem1, recv_sem1, send_sem2, recv_sem2,
):
    R, C = lax.axis_index("row"), lax.axis_index("col")
    plane, mine = R % 4, (R // 4) * 4 + C

    def device(d):
        return {"row": (d // 4) * 4 + plane, "col": d % 4}

    up, down = (R + 31) % 32, (R + 1) % 32
    left, right = (C + 3) % 4, (C + 1) % 4

    barrier = pltpu.get_barrier_semaphore()

    def greet(n, carry):
        pl.semaphore_signal(barrier, inc=1, device_id=device((mine + n) % 32), device_id_type=MESH)
        return carry

    lax.fori_loop(1, 32, greet, 0)
    for r in (up, down):
        for c in (left, C, right):
            pl.semaphore_signal(barrier, inc=1, device_id={"row": r, "col": c}, device_id_type=MESH)

    row16 = lax.broadcasted_iota(jnp.int32, (32, 16, WIDTH), 1)
    edge_l[...] = jnp.sum(
        jnp.where(row16 == 0, image[:, 0:16, :].astype(F32), 0.0), axis=1
    ).astype(BF)
    edge_r[...] = jnp.sum(
        jnp.where(row16 == 15, image[:, 112:128, :].astype(F32), 0.0), axis=1
    ).astype(BF)

    pl.semaphore_wait(barrier, 37)

    def halo_copies():
        plan = (
            (image.at[31], halo_tb.at[0], down, C),
            (image.at[0], halo_tb.at[1], up, C),
            (edge_r, halo_l.at[pl.ds(16, 32)], R, right),
            (edge_l, halo_r.at[pl.ds(16, 32)], R, left),
            (edge_r.at[pl.ds(16, 16)], halo_l.at[pl.ds(0, 16)], down, right),
            (edge_r.at[pl.ds(0, 16)], halo_l.at[pl.ds(48, 16)], up, right),
            (edge_l.at[pl.ds(16, 16)], halo_r.at[pl.ds(0, 16)], down, left),
            (edge_l.at[pl.ds(0, 16)], halo_r.at[pl.ds(48, 16)], up, left),
        )
        return [
            pltpu.make_async_remote_copy(
                src_ref=src, dst_ref=dst, send_sem=halo_send.at[n], recv_sem=halo_recv.at[n],
                device_id={"row": r, "col": c}, device_id_type=MESH,
            )
            for n, (src, dst, r, c) in enumerate(plan)
        ]

    halos = halo_copies()
    for copy in halos:
        copy.start()
    perms[0] = perm_image()
    perms[1] = perm_image_back()
    perms[2] = perm_swap()
    perms[3] = perm_grid()
    perms[4] = perm_grid_back()
    row_head = (lax.broadcasted_iota(jnp.int32, (256, 128), 0) // 16) % 4
    lane_head = lax.broadcasted_iota(jnp.int32, (256, 128), 1) // HEAD_DIM
    ones[...] = (row_head == lane_head).astype(F32).astype(BF)
    w_half[...] = w_expand[...] * jnp.asarray(0.5, BF)
    for n in range(9):
        tap = depth[n // 3, pl.ds(n % 3, 1), :].astype(F32) * 0.5
        taps[n] = jnp.broadcast_to(tap, (16, EXPANDED)).astype(BF)

    def expand(tokens, row0, row1, keep):
        x = dot(perms[0], tokens)
        if keep is not None:
            image_p[keep] = x.astype(BF)
        normed = layer_norm(x).astype(BF)
        for n in range(4):
            ch = slice(256 * n, 256 * n + 256)
            h = gelu_of_half(dot(normed, w_half[:, ch])).astype(BF)
            hidden[row0, 1:9, :, ch] = h[:128].reshape(8, 16, 256)
            hidden[row1, 1:9, :, ch] = h[128:].reshape(8, 16, 256)

    def expand_image(b):
        rows = image[pl.ds(2 * b, 2)].reshape(256, WIDTH)
        expand(rows, 2 * b + 1, 2 * b + 2, b)

    def expand_images(first, last):
        def each(b, carry):
            expand_image(b)
            return carry

        lax.fori_loop(first, last, each, 0)

    expand_images(0, 16)
    for copy in halos:
        copy.wait()

    row64 = lax.broadcasted_iota(jnp.int32, (64, WIDTH), 0)
    off_grid = ((row64 <= 15) & (R == 0)) | ((row64 >= 48) & (R == 31))
    for halo, off, hid in ((halo_l, C == 0, hid_l), (halo_r, C == 3, hid_r)):
        x = jnp.where(off_grid | off, 0.0, halo[...].astype(F32))
        hid[...] = gelu_of_half(dot(layer_norm(x).astype(BF), w_half[...]))
    row256 = lax.broadcasted_iota(jnp.int32, (256, WIDTH), 0)
    off_grid = ((row256 < 128) & (R == 0)) | ((row256 >= 128) & (R == 31))
    x = jnp.where(off_grid, 0.0, halo_tb[...].reshape(256, WIDTH).astype(F32)).astype(BF)
    expand(x, 0, 33, None)

    row_s = lax.broadcasted_iota(jnp.int32, (16, EXPANDED), 0)

    def edges(r):
        from_left = pltpu.roll(hidden[r, 8].astype(F32), 1, 0)
        hidden[r, 0] = jnp.where(row_s == 0, hid_l[pl.ds(15 + r, 1), :], from_left).astype(BF)
        from_right = pltpu.roll(hidden[r, 1].astype(F32), 15, 0)
        hidden[r, 9] = jnp.where(row_s == 15, hid_r[pl.ds(15 + r, 1), :], from_right).astype(BF)

    for r in range(2):
        edges(r)

    def convolve(b):
        for row in range(2):
            for n in range(8):
                ch = slice(128 * n, 128 * n + 128)
                total = None
                for dr in range(3):
                    for dc in range(3):
                        term = hidden[2 * b + row + dr, dc : dc + 8, :, ch] * taps[3 * dr + dc, :, ch]
                        total = term if total is None else total + term
                act[128 * row : 128 * row + 128, ch] = gelu_of_half(total).reshape(128, 128)
        update = dot(act[...], w_project[...])
        return (image_p[b].astype(F32) + update).astype(BF)

    def exchange(src_of, dst_of, send_sem, recv_sem):
        own = pltpu.make_async_copy(src_of(mine), dst_of(mine), recv_sem)
        own.start()

        def send(n, carry):
            d = (mine + n) % 32
            pltpu.make_async_remote_copy(
                src_ref=src_of(d), dst_ref=dst_of(mine), send_sem=send_sem, recv_sem=recv_sem,
                device_id=device(d), device_id_type=MESH,
            ).start()
            return carry

        lax.fori_loop(1, 32, send, 0)

    def image_part(buf, k):
        return lambda d: buf.at[8 * k + d // 4, pl.ds(2 * (d % 4), 2)]

    def grid_part(buf, k):
        return lambda d: buf.at[k, d]

    def reorder_out(perm, store):
        for n in range(4):
            block = res[:, 16 * n : 16 * n + 16, :].reshape(256, WIDTH)
            store(n, dot(perm, block).astype(BF))

    def band(k, carry):
        @pl.when(k < 4)
        def _():
            def rows(n, carry):
                b = 4 * k + n

                edges(2 * b + 2)
                edges(2 * b + 3)
                first = convolve(b)
                swapped = dot(perms[2], first).reshape(16, 16, WIDTH)
                tok[:, pl.ds(pl.multiple_of(16 * n, 16), 16), :] = swapped
                return carry

            lax.fori_loop(0, 4, rows, 0)
            attention(tok, res, b_qkv, b_out, b_bias, ones)

            def store(n, x):
                send1[pl.ds(8 * k + 2 * n, 2)] = x.reshape(2, 8, 16, WIDTH)

            reorder_out(perms[2], store)
            exchange(image_part(send1, k), grid_part(recv1, k), send_sem1.at[k], recv_sem1.at[k])

        @pl.when(k >= 1)
        def _():
            g = k - 1
            pltpu.make_async_copy(recv1.at[g], recv1.at[g], recv_sem1.at[g]).wait()
            for n in range(4):
                x = recv1[g, 8 * n : 8 * n + 8].reshape(256, WIDTH)
                tok[:, 16 * n : 16 * n + 16, :] = dot(perms[3], x).reshape(16, 16, WIDTH)
            attention(tok, res, g_qkv, g_out, g_bias, ones)

            def store(n, x):
                send2[g, 8 * n : 8 * n + 8] = x.reshape(8, 2, 16, WIDTH)

            reorder_out(perms[4], store)
            exchange_back(g)

        return carry

    def exchange_back(g):
        own = pltpu.make_async_copy(send2.at[g, mine], image_part(recv2, g)(mine), recv_sem2.at[g])
        own.start()

        def send(n, carry):
            d = (mine + n) % 32
            pltpu.make_async_remote_copy(
                src_ref=send2.at[g, d], dst_ref=image_part(recv2, g)(mine),
                send_sem=send_sem2.at[g], recv_sem=recv_sem2.at[g],
                device_id=device(d), device_id_type=MESH,
            ).start()
            return carry

        lax.fori_loop(1, 32, send, 0)

    lax.fori_loop(0, 5, band, 0)

    def finish(g, carry):
        view = recv2.at[pl.ds(8 * g, 8)]
        pltpu.make_async_copy(view, view, recv_sem2.at[g]).wait()
        for n in range(4):
            x = recv2[pl.ds(8 * g + 2 * n, 2)].reshape(256, WIDTH)
            result[pl.ds(8 * g + 2 * n, 2)] = dot(perms[1], x).astype(BF).reshape(2, 128, WIDTH)
        return carry

    lax.fori_loop(0, 4, finish, 0)

    def drain(g, carry):
        part = send2.at[g, pl.ds(0, 31)]
        pltpu.make_async_copy(part, part, send_sem1.at[g]).wait()
        pltpu.make_async_copy(part, part, send_sem2.at[g]).wait()
        return carry

    lax.fori_loop(0, 4, drain, 0)


def in_tiles(bias):
    tiled = (bias * LOG2E).reshape(2, 4, 64, 4, 16).transpose(0, 2, 3, 1, 4)
    return tiled.reshape(2, 64, 256)


def on_device(image, w_expand, depth, w_project, b_qkv, b_out, b_bias, g_qkv, g_out, g_bias):
    vmem = pl.BlockSpec(memory_space=pltpu.VMEM)
    dma = pltpu.SemaphoreType.DMA
    return pl.pallas_call(
        kernel,
        out_shape=jax.ShapeDtypeStruct(image.shape, BF),
        in_specs=[vmem] * 10,
        out_specs=vmem,
        scratch_shapes=[
            pltpu.VMEM((2, 128, WIDTH), BF),
            pltpu.VMEM((64, WIDTH), BF),
            pltpu.VMEM((64, WIDTH), BF),
            pltpu.VMEM((32, WIDTH), BF),
            pltpu.VMEM((32, WIDTH), BF),
            pltpu.VMEM((32, 8, 16, WIDTH), BF),
            pltpu.VMEM((4, 32, 2, 16, WIDTH), BF),
            pltpu.VMEM((4, 32, 2, 16, WIDTH), BF),
            pltpu.VMEM((32, 8, 16, WIDTH), BF),
            pltpu.VMEM((34, 10, 16, EXPANDED), BF),
            pltpu.VMEM((16, 256, WIDTH), BF),
            pltpu.VMEM((WIDTH, EXPANDED), BF),
            pltpu.VMEM((9, 16, EXPANDED), BF),
            pltpu.VMEM((64, EXPANDED), F32),
            pltpu.VMEM((64, EXPANDED), F32),
            pltpu.VMEM((256, EXPANDED), BF),
            pltpu.VMEM((16, 64, WIDTH), F32),
            pltpu.VMEM((16, 64, WIDTH), BF),
            pltpu.VMEM((5, 256, 256), BF),
            pltpu.VMEM((256, 128), BF),
            dma((8,)),
            dma((8,)),
            dma((4,)),
            dma((4,)),
            dma((4,)),
            dma((4,)),
        ],
        compiler_params=pltpu.CompilerParams(
            collective_id=0, has_side_effects=True, vmem_limit_bytes=56 << 20
        ),
    )(
        image, w_expand, depth, w_project, b_qkv, b_out, in_tiles(b_bias),
        g_qkv, g_out, in_tiles(g_bias),
    )


def solution(mesh):
    in_specs = (P("row", "col", None),) + (P(),) * 9
    return jax.shard_map(
        on_device, mesh=mesh, in_specs=in_specs, out_specs=P("row", "col", None), check_vma=False
    )
```

```python
import functools

import jax
import jax.numpy as jnp
from jax import lax
from jax.experimental import pallas as pl
from jax.experimental.pallas import tpu as pltpu
from jax.sharding import PartitionSpec as P

MESH = pl.DeviceIdType.MESH
HEADS = 8
HEAD_DIM = 32
WIDTH = 256
EXPANDED = 1024
LOG2E = 1.4426950408889634
ROOT2 = 1.4142135623730951
BF = jnp.bfloat16
F32 = jnp.float32


def dot(a, b):
    return jnp.dot(a, b, preferred_element_type=F32)


def dot_nt(a, b):
    return lax.dot_general(a, b, (((1,), (1,)), ((), ())), preferred_element_type=F32)


def layer_norm(v):
    mean = jnp.mean(v, axis=-1, keepdims=True)
    cen = v - mean
    var = jnp.mean(cen * cen, axis=-1, keepdims=True)
    return cen * lax.rsqrt(var + 1e-5)


def gelu_of_half(z):
    return z + z * lax.erf(z * jnp.asarray(ROOT2, z.dtype))


def perm_image():
    out = lax.broadcasted_iota(jnp.int32, (256, 256), 0)
    src = lax.broadcasted_iota(jnp.int32, (256, 256), 1)
    want = (out & 128) | ((out & 15) << 3) | ((out >> 4) & 7)
    return (src == want).astype(F32).astype(BF)


def perm_image_back():
    out = lax.broadcasted_iota(jnp.int32, (256, 256), 0)
    src = lax.broadcasted_iota(jnp.int32, (256, 256), 1)
    want = (out & 128) | ((out & 7) << 4) | ((out >> 3) & 15)
    return (src == want).astype(F32).astype(BF)


def perm_swap():
    out = lax.broadcasted_iota(jnp.int32, (256, 256), 0)
    src = lax.broadcasted_iota(jnp.int32, (256, 256), 1)
    want = ((out & 15) << 4) | (out >> 4)
    return (src == want).astype(F32).astype(BF)


def perm_grid():
    out = lax.broadcasted_iota(jnp.int32, (256, 256), 0)
    src = lax.broadcasted_iota(jnp.int32, (256, 256), 1)
    group, pos = out >> 4, out & 15
    j0, s = group >> 3, group & 7
    want = ((pos >> 1) << 5) | (j0 << 4) | ((pos & 1) << 3) | s
    return (src == want).astype(F32).astype(BF)


def perm_grid_back():
    out = lax.broadcasted_iota(jnp.int32, (256, 256), 0)
    src = lax.broadcasted_iota(jnp.int32, (256, 256), 1)
    msg, j0, jl, s = out >> 5, (out >> 4) & 1, (out >> 3) & 1, out & 7
    want = (((j0 << 3) | s) << 4) | (msg << 1) | jl
    return (src == want).astype(F32).astype(BF)


def spread(x, masks):
    return jnp.concatenate(
        [x[16 * t : 16 * t + 16] * masks[h] for t in range(4) for h in range(4)], axis=0
    )


def bias_tiles(bias, out):
    lane = lax.broadcasted_iota(jnp.int32, (64, 128), 1)
    pad = jnp.zeros((64, 64), F32)
    for n in range(2):
        wide = [jnp.concatenate([bias[4 * n + h], pad], axis=1) * LOG2E for h in range(4)]
        for pair in range(2):
            total = jnp.zeros((64, 128), F32)
            for t in range(2):
                for h in range(4):
                    to = 64 * t + 16 * h
                    moved = pltpu.roll(wide[h], (to - 16 * (2 * pair + t)) % 128, 1)
                    total = jnp.where((lane >= to) & (lane < to + 16), moved, total)
            out[n, :, 128 * pair : 128 * pair + 128] = total


def attention(tok, res, w_qkv, w_out, bias, ones):
    lane = lax.broadcasted_iota(jnp.int32, (256, 128), 1)
    high = lane >= 64
    mlane = lax.broadcasted_iota(jnp.int32, (16, 128), 1)
    masks = [(mlane // HEAD_DIM == h).astype(F32).astype(BF) for h in range(4)]
    groups = [slice(64 * g, 64 * g + 64) for g in range(4)]
    halves = (slice(0, 128), slice(128, 256))

    def step(c, carry):
        t = tok[pl.ds(4 * c, 4)].reshape(256, WIDTH)
        normed = layer_norm(t).astype(BF)
        qkv = dot(normed, w_qkv[...])
        q = (qkv[:, :WIDTH] * (LOG2E / HEAD_DIM**0.5)).astype(BF)
        k = qkv[:, WIDTH : 2 * WIDTH].astype(BF)
        v = qkv[:, 2 * WIDTH :].astype(BF)
        tiles, tops = [], []
        for n, half in enumerate(halves):
            z = jnp.concatenate(
                [dot_nt(q[g, half], spread(k[g, half], masks)) + bias[n] for g in groups], axis=0
            )
            tiles.append((z[:, :128], z[:, 128:]))
            tops.append(jnp.maximum(z[:, :128], z[:, 128:]))
        m = jnp.maximum(
            jnp.where(high, tops[0], tops[1]), pltpu.roll(jnp.where(high, tops[1], tops[0]), 64, 1)
        )
        for bit in (8, 4, 2, 1):
            m = jnp.maximum(m, jnp.take_along_axis(m, lane ^ bit, axis=1))
        other = pltpu.roll(m, 64, 1)
        tops = (jnp.where(high, m, other), jnp.where(high, other, m))
        mixed = []
        for n, half in enumerate(halves):
            p = jnp.concatenate([jnp.exp2(x - tops[n]).astype(BF) for x in tiles[n]], axis=1)
            den = dot(p, ones[...])
            num = jnp.concatenate([dot(p[g], spread(v[g, half], masks)) for g in groups], axis=0)
            mixed.append((num / den).astype(BF))
        out = dot(jnp.concatenate(mixed, axis=1), w_out[...]) + t
        res[pl.ds(4 * c, 4)] = out.astype(BF).reshape(4, 64, WIDTH)
        return carry

    lax.fori_loop(0, 4, step, 0, unroll=4)


def kernel(
    image, w_expand, depth, w_project, b_qkv, b_out, b_bias, g_qkv, g_out, g_bias,
    result,
    halo_tb, halo_l, halo_r, edge_l, edge_r, send1, recv1, send2, recv2,
    hidden, image_p, w_half, taps, hid_l, hid_r, act0, act1, tok, res, perms, ones, bias_w, bias_g,
    halo_send, halo_recv, send_sem1, recv_sem1, send_sem2, recv_sem2,
):
    R, C = lax.axis_index("row"), lax.axis_index("col")
    mine = (R // 4) * 4 + C

    def peers():
        out = []
        for i in (4, 3, 5, 2, 6, 1, 7, 0):
            row = (R + 4 * i) % 32
            for c in (2, 3, 1, 0):
                if i or c:
                    col = (C + c) % 4
                    out.append(((row // 4) * 4 + col, {"row": row, "col": col}))
        return out

    up, down = (R + 31) % 32, (R + 1) % 32
    left, right = (C + 3) % 4, (C + 1) % 4

    barrier = pltpu.get_barrier_semaphore()

    for _, to in peers():
        pl.semaphore_signal(barrier, inc=1, device_id=to, device_id_type=MESH)
    for r in (up, down):
        for c in (left, C, right):
            pl.semaphore_signal(barrier, inc=1, device_id={"row": r, "col": c}, device_id_type=MESH)

    row16 = lax.broadcasted_iota(jnp.int32, (32, 16, WIDTH), 1)
    edge_l[...] = jnp.sum(
        jnp.where(row16 == 0, image[:, 0:16, :].astype(F32), 0.0), axis=1
    ).astype(BF)
    edge_r[...] = jnp.sum(
        jnp.where(row16 == 15, image[:, 112:128, :].astype(F32), 0.0), axis=1
    ).astype(BF)

    pl.semaphore_wait(barrier, 37)

    def halo_copies():
        plan = (
            (image.at[31], halo_tb.at[0], down, C),
            (image.at[0], halo_tb.at[1], up, C),
            (edge_r, halo_l.at[pl.ds(16, 32)], R, right),
            (edge_l, halo_r.at[pl.ds(16, 32)], R, left),
            (edge_r.at[pl.ds(16, 16)], halo_l.at[pl.ds(0, 16)], down, right),
            (edge_r.at[pl.ds(0, 16)], halo_l.at[pl.ds(48, 16)], up, right),
            (edge_l.at[pl.ds(16, 16)], halo_r.at[pl.ds(0, 16)], down, left),
            (edge_l.at[pl.ds(0, 16)], halo_r.at[pl.ds(48, 16)], up, left),
        )
        return [
            pltpu.make_async_remote_copy(
                src_ref=src, dst_ref=dst, send_sem=halo_send.at[n], recv_sem=halo_recv.at[n],
                device_id={"row": r, "col": c}, device_id_type=MESH,
            )
            for n, (src, dst, r, c) in enumerate(plan)
        ]

    halos = halo_copies()
    for copy in halos:
        copy.start()
    perms[0] = perm_image()
    perms[1] = perm_image_back()
    perms[2] = perm_swap()
    perms[3] = perm_grid()
    perms[4] = perm_grid_back()
    row_head = (lax.broadcasted_iota(jnp.int32, (256, 128), 0) // 16) % 4
    lane_head = lax.broadcasted_iota(jnp.int32, (256, 128), 1) // HEAD_DIM
    ones[...] = (row_head == lane_head).astype(F32).astype(BF)
    bias_tiles(b_bias, bias_w)
    bias_tiles(g_bias, bias_g)
    w_half[...] = w_expand[...] * jnp.asarray(0.5, BF)
    for n in range(9):
        tap = depth[n // 3, pl.ds(n % 3, 1), :].astype(F32) * 0.5
        taps[n] = jnp.broadcast_to(tap, (16, EXPANDED)).astype(BF)

    def expand(tokens, row0, row1, keep):
        x = dot(perms[0], tokens)
        if keep is not None:
            image_p[keep] = x.astype(BF)
        normed = layer_norm(x).astype(BF)
        for n in range(4):
            ch = slice(256 * n, 256 * n + 256)
            h = gelu_of_half(dot(normed, w_half[:, ch])).astype(BF)
            hidden[row0, 1:9, :, ch] = h[:128].reshape(8, 16, 256)
            hidden[row1, 1:9, :, ch] = h[128:].reshape(8, 16, 256)

    def expand_image(b):
        rows = image[pl.ds(2 * b, 2)].reshape(256, WIDTH)
        expand(rows, 2 * b + 1, 2 * b + 2, b)

    def expand_images(first, last):
        def each(b, carry):
            expand_image(b)
            return carry

        lax.fori_loop(first, last, each, 0)

    expand_images(0, 16)
    for copy in halos:
        copy.wait()

    row64 = lax.broadcasted_iota(jnp.int32, (64, WIDTH), 0)
    off_grid = ((row64 <= 15) & (R == 0)) | ((row64 >= 48) & (R == 31))
    for halo, off, hid in ((halo_l, C == 0, hid_l), (halo_r, C == 3, hid_r)):
        x = jnp.where(off_grid | off, 0.0, halo[...].astype(F32))
        hid[...] = gelu_of_half(dot(layer_norm(x).astype(BF), w_half[...]))
    row256 = lax.broadcasted_iota(jnp.int32, (256, WIDTH), 0)
    off_grid = ((row256 < 128) & (R == 0)) | ((row256 >= 128) & (R == 31))
    x = jnp.where(off_grid, 0.0, halo_tb[...].reshape(256, WIDTH).astype(F32)).astype(BF)
    expand(x, 0, 33, None)

    row_s = lax.broadcasted_iota(jnp.int32, (16, EXPANDED), 0)

    def edges(r):
        from_left = pltpu.roll(hidden[r, 8].astype(F32), 1, 0)
        hidden[r, 0] = jnp.where(row_s == 0, hid_l[pl.ds(15 + r, 1), :], from_left).astype(BF)
        from_right = pltpu.roll(hidden[r, 1].astype(F32), 15, 0)
        hidden[r, 9] = jnp.where(row_s == 15, hid_r[pl.ds(15 + r, 1), :], from_right).astype(BF)

    def all_edges(r, carry):
        edges(r)
        return carry

    lax.fori_loop(0, 34, all_edges, 0)

    def convolve(b, act):
        for row in range(2):
            for n in range(8):
                ch = slice(128 * n, 128 * n + 128)
                total = None
                for dr in range(3):
                    for dc in range(3):
                        term = hidden[2 * b + row + dr, dc : dc + 8, :, ch] * taps[3 * dr + dc, :, ch]
                        total = term if total is None else total + term
                act[128 * row : 128 * row + 128, ch] = gelu_of_half(total).reshape(128, 128)

    def project(b, n, act):
        update = dot(act[...], w_project[...])
        first = (image_p[b].astype(F32) + update).astype(BF)
        tok[:, 16 * n : 16 * n + 16, :] = dot(perms[2], first).reshape(16, 16, WIDTH)

    def exchange(src_of, dst_of, send_sem, recv_sem):
        own = pltpu.make_async_copy(src_of(mine), dst_of(mine), recv_sem)
        own.start()

        for d, to in peers():
            pltpu.make_async_remote_copy(
                src_ref=src_of(d), dst_ref=dst_of(mine), send_sem=send_sem, recv_sem=recv_sem,
                device_id=to, device_id_type=MESH,
            ).start()

    def image_part(buf, k):
        return lambda d: buf.at[8 * k + d // 4, pl.ds(2 * (d % 4), 2)]

    def grid_part(buf, k):
        return lambda d: buf.at[k, d]

    def reorder_out(perm, store):
        for n in range(4):
            block = res[:, 16 * n : 16 * n + 16, :].reshape(256, WIDTH)
            store(n, dot(perm, block).astype(BF))

    def band(k, carry):
        @pl.when(k < 4)
        def _():
            acts = (act0, act1)
            for n in range(4):
                convolve(4 * k + n, acts[n % 2])
                if n:
                    project(4 * k + n - 1, n - 1, acts[(n - 1) % 2])
            project(4 * k + 3, 3, acts[1])
            attention(tok, res, b_qkv, b_out, bias_w, ones)

            def store(n, x):
                send1[pl.ds(8 * k + 2 * n, 2)] = x.reshape(2, 8, 16, WIDTH)

            reorder_out(perms[2], store)
            exchange(image_part(send1, k), grid_part(recv1, k), send_sem1.at[k], recv_sem1.at[k])

        @pl.when(k >= 1)
        def _():
            g = k - 1
            pltpu.make_async_copy(recv1.at[g], recv1.at[g], recv_sem1.at[g]).wait()
            for n in range(4):
                x = recv1[g, 8 * n : 8 * n + 8].reshape(256, WIDTH)
                tok[:, 16 * n : 16 * n + 16, :] = dot(perms[3], x).reshape(16, 16, WIDTH)
            attention(tok, res, g_qkv, g_out, bias_g, ones)

            def store(n, x):
                send2[g, 8 * n : 8 * n + 8] = x.reshape(8, 2, 16, WIDTH)

            reorder_out(perms[4], store)
            exchange_back(g)

        return carry

    def exchange_back(g):
        own = pltpu.make_async_copy(send2.at[g, mine], image_part(recv2, g)(mine), recv_sem2.at[g])
        own.start()

        for d, to in peers():
            pltpu.make_async_remote_copy(
                src_ref=send2.at[g, d], dst_ref=image_part(recv2, g)(mine),
                send_sem=send_sem2.at[g], recv_sem=recv_sem2.at[g],
                device_id=to, device_id_type=MESH,
            ).start()

    lax.fori_loop(0, 5, band, 0)

    def finish(g, carry):
        view = recv2.at[pl.ds(8 * g, 8)]
        pltpu.make_async_copy(view, view, recv_sem2.at[g]).wait()
        for n in range(4):
            x = recv2[pl.ds(8 * g + 2 * n, 2)].reshape(256, WIDTH)
            result[pl.ds(8 * g + 2 * n, 2)] = dot(perms[1], x).astype(BF).reshape(2, 128, WIDTH)
        return carry

    lax.fori_loop(0, 4, finish, 0)

    def drain(g, carry):
        part = send2.at[g, pl.ds(0, 31)]
        pltpu.make_async_copy(part, part, send_sem1.at[g]).wait()
        pltpu.make_async_copy(part, part, send_sem2.at[g]).wait()
        return carry

    lax.fori_loop(0, 4, drain, 0)


def on_device(image, w_expand, depth, w_project, b_qkv, b_out, b_bias, g_qkv, g_out, g_bias):
    vmem = pl.BlockSpec(memory_space=pltpu.VMEM)
    dma = pltpu.SemaphoreType.DMA
    return pl.pallas_call(
        kernel,
        out_shape=jax.ShapeDtypeStruct(image.shape, BF),
        in_specs=[vmem] * 10,
        out_specs=vmem,
        scratch_shapes=[
            pltpu.VMEM((2, 128, WIDTH), BF),
            pltpu.VMEM((64, WIDTH), BF),
            pltpu.VMEM((64, WIDTH), BF),
            pltpu.VMEM((32, WIDTH), BF),
            pltpu.VMEM((32, WIDTH), BF),
            pltpu.VMEM((32, 8, 16, WIDTH), BF),
            pltpu.VMEM((4, 32, 2, 16, WIDTH), BF),
            pltpu.VMEM((4, 32, 2, 16, WIDTH), BF),
            pltpu.VMEM((32, 8, 16, WIDTH), BF),
            pltpu.VMEM((34, 10, 16, EXPANDED), BF),
            pltpu.VMEM((16, 256, WIDTH), BF),
            pltpu.VMEM((WIDTH, EXPANDED), BF),
            pltpu.VMEM((9, 16, EXPANDED), BF),
            pltpu.VMEM((64, EXPANDED), F32),
            pltpu.VMEM((64, EXPANDED), F32),
            pltpu.VMEM((256, EXPANDED), BF),
            pltpu.VMEM((256, EXPANDED), BF),
            pltpu.VMEM((16, 64, WIDTH), F32),
            pltpu.VMEM((16, 64, WIDTH), BF),
            pltpu.VMEM((5, 256, 256), BF),
            pltpu.VMEM((256, 128), BF),
            pltpu.VMEM((2, 64, 256), F32),
            pltpu.VMEM((2, 64, 256), F32),
            dma((8,)),
            dma((8,)),
            dma((4,)),
            dma((4,)),
            dma((4,)),
            dma((4,)),
        ],
        compiler_params=pltpu.CompilerParams(
            collective_id=0, has_side_effects=True, vmem_limit_bytes=56 << 20
        ),
    )(
        image, w_expand, depth, w_project, b_qkv, b_out, b_bias, g_qkv, g_out, g_bias
    )


def solution(mesh):
    in_specs = (P("row", "col", None),) + (P(),) * 9
    return jax.shard_map(
        on_device, mesh=mesh, in_specs=in_specs, out_specs=P("row", "col", None), check_vma=False
    )
```

```python
import functools

import jax
import jax.numpy as jnp
from jax import lax
from jax.experimental import pallas as pl
from jax.experimental.pallas import tpu as pltpu
from jax.sharding import PartitionSpec as P

MESH = pl.DeviceIdType.MESH
HEADS = 8
HEAD_DIM = 32
WIDTH = 256
EXPANDED = 1024
LOG2E = 1.4426950408889634
ROOT2 = 1.4142135623730951
BF = jnp.bfloat16
F32 = jnp.float32


def dot(a, b):
    return jnp.dot(a, b, preferred_element_type=F32)


def dot_nt(a, b):
    return lax.dot_general(a, b, (((1,), (1,)), ((), ())), preferred_element_type=F32)


def layer_norm(v):
    mean = jnp.mean(v, axis=-1, keepdims=True)
    cen = v - mean
    var = jnp.mean(cen * cen, axis=-1, keepdims=True)
    return cen * lax.rsqrt(var + 1e-5)


def gelu_of_half(z):
    return z + z * lax.erf(z * jnp.asarray(ROOT2, z.dtype))


def perm_image():
    out = lax.broadcasted_iota(jnp.int32, (256, 256), 0)
    src = lax.broadcasted_iota(jnp.int32, (256, 256), 1)
    want = (out & 128) | ((out & 15) << 3) | ((out >> 4) & 7)
    return (src == want).astype(F32).astype(BF)


def perm_image_back():
    out = lax.broadcasted_iota(jnp.int32, (256, 256), 0)
    src = lax.broadcasted_iota(jnp.int32, (256, 256), 1)
    want = (out & 128) | ((out & 7) << 4) | ((out >> 3) & 15)
    return (src == want).astype(F32).astype(BF)


def perm_swap():
    out = lax.broadcasted_iota(jnp.int32, (256, 256), 0)
    src = lax.broadcasted_iota(jnp.int32, (256, 256), 1)
    want = ((out & 15) << 4) | (out >> 4)
    return (src == want).astype(F32).astype(BF)


def perm_grid():
    out = lax.broadcasted_iota(jnp.int32, (256, 256), 0)
    src = lax.broadcasted_iota(jnp.int32, (256, 256), 1)
    group, pos = out >> 4, out & 15
    j0, s = group >> 3, group & 7
    want = ((pos >> 1) << 5) | (j0 << 4) | ((pos & 1) << 3) | s
    return (src == want).astype(F32).astype(BF)


def perm_grid_back():
    out = lax.broadcasted_iota(jnp.int32, (256, 256), 0)
    src = lax.broadcasted_iota(jnp.int32, (256, 256), 1)
    msg, j0, jl, s = out >> 5, (out >> 4) & 1, (out >> 3) & 1, out & 7
    want = (((j0 << 3) | s) << 4) | (msg << 1) | jl
    return (src == want).astype(F32).astype(BF)


def spread(x, masks):
    return jnp.concatenate(
        [x[16 * t : 16 * t + 16] * masks[h] for t in range(4) for h in range(4)], axis=0
    )


def bias_tiles(bias, out):
    lane = lax.broadcasted_iota(jnp.int32, (64, 128), 1)
    pad = jnp.zeros((64, 64), F32)
    for n in range(2):
        wide = [jnp.concatenate([bias[4 * n + h], pad], axis=1) * LOG2E for h in range(4)]
        for pair in range(2):
            total = jnp.zeros((64, 128), F32)
            for t in range(2):
                for h in range(4):
                    to = 64 * t + 16 * h
                    moved = pltpu.roll(wide[h], (to - 16 * (2 * pair + t)) % 128, 1)
                    total = jnp.where((lane >= to) & (lane < to + 16), moved, total)
            out[n, :, 128 * pair : 128 * pair + 128] = total


def attention(tok, res, w_qkv, w_out, bias, ones):
    lane = lax.broadcasted_iota(jnp.int32, (256, 128), 1)
    high = lane >= 64
    mlane = lax.broadcasted_iota(jnp.int32, (16, 128), 1)
    masks = [(mlane // HEAD_DIM == h).astype(F32).astype(BF) for h in range(4)]
    groups = [slice(64 * g, 64 * g + 64) for g in range(4)]
    halves = (slice(0, 128), slice(128, 256))

    def project(c):
        t = tok[pl.ds(4 * c, 4)].reshape(256, WIDTH)
        qkv = dot(layer_norm(t).astype(BF), w_qkv[...])
        q = (qkv[:, :WIDTH] * (LOG2E / HEAD_DIM**0.5)).astype(BF)
        return q, qkv[:, WIDTH : 2 * WIDTH].astype(BF), qkv[:, 2 * WIDTH :].astype(BF)

    def scores(q, k, v):
        tiles = []
        for n, half in enumerate(halves):
            z = jnp.concatenate(
                [dot_nt(q[g, half], spread(k[g, half], masks)) + bias[n] for g in groups], axis=0
            )
            tiles.append((z[:, :128], z[:, 128:]))
        return v, tiles

    def weigh(v, tiles):
        tops = [jnp.maximum(*pair) for pair in tiles]
        m = jnp.maximum(
            jnp.where(high, tops[0], tops[1]), pltpu.roll(jnp.where(high, tops[1], tops[0]), 64, 1)
        )
        for bit in (8, 4, 2, 1):
            m = jnp.maximum(m, jnp.take_along_axis(m, lane ^ bit, axis=1))
        other = pltpu.roll(m, 64, 1)
        tops = (jnp.where(high, m, other), jnp.where(high, other, m))
        return v, [
            jnp.concatenate([jnp.exp2(x - tops[n]).astype(BF) for x in tiles[n]], axis=1)
            for n in range(2)
        ]

    def mix(c, v, weights):
        mixed = []
        for n, half in enumerate(halves):
            p = weights[n]
            den = dot(p, ones[...])
            num = jnp.concatenate([dot(p[g], spread(v[g, half], masks)) for g in groups], axis=0)
            mixed.append((num / den).astype(BF))
        out = dot(jnp.concatenate(mixed, axis=1), w_out[...])
        out = out + tok[pl.ds(4 * c, 4)].reshape(256, WIDTH)
        res[pl.ds(4 * c, 4)] = out.astype(BF).reshape(4, 64, WIDTH)

    first, second, third = {}, {}, {}
    for i in range(7):
        if i < 4:
            first[i] = project(i)
        if 0 <= i - 1 < 4:
            second[i - 1] = scores(*first[i - 1])
        if 0 <= i - 2 < 4:
            third[i - 2] = weigh(*second[i - 2])
        if 0 <= i - 3 < 4:
            mix(i - 3, *third[i - 3])


def kernel(
    image, w_expand, depth, w_project, b_qkv, b_out, b_bias, g_qkv, g_out, g_bias,
    result,
    halo_tb, halo_l, halo_r, edge_l, edge_r, send1, recv1, send2, recv2,
    hidden, image_p, w_half, taps, hid_l, hid_r, act0, act1, tok, res, perms, ones, bias_w, bias_g,
    halo_send, halo_recv, send_sem1, recv_sem1, send_sem2, recv_sem2,
):
    R, C = lax.axis_index("row"), lax.axis_index("col")
    mine = (R // 4) * 4 + C

    def peers():
        out = []
        for i in (4, 3, 5, 2, 6, 1, 7, 0):
            row = (R + 4 * i) % 32
            for c in (2, 3, 1, 0):
                if i or c:
                    col = (C + c) % 4
                    out.append(((row // 4) * 4 + col, {"row": row, "col": col}))
        return out

    up, down = (R + 31) % 32, (R + 1) % 32
    left, right = (C + 3) % 4, (C + 1) % 4

    barrier = pltpu.get_barrier_semaphore()

    for _, to in peers():
        pl.semaphore_signal(barrier, inc=1, device_id=to, device_id_type=MESH)
    for r in (up, down):
        for c in (left, C, right):
            pl.semaphore_signal(barrier, inc=1, device_id={"row": r, "col": c}, device_id_type=MESH)

    row16 = lax.broadcasted_iota(jnp.int32, (32, 16, WIDTH), 1)
    edge_l[...] = jnp.sum(
        jnp.where(row16 == 0, image[:, 0:16, :].astype(F32), 0.0), axis=1
    ).astype(BF)
    edge_r[...] = jnp.sum(
        jnp.where(row16 == 15, image[:, 112:128, :].astype(F32), 0.0), axis=1
    ).astype(BF)

    pl.semaphore_wait(barrier, 37)

    def halo_copies():
        plan = (
            (image.at[31], halo_tb.at[0], down, C),
            (image.at[0], halo_tb.at[1], up, C),
            (edge_r, halo_l.at[pl.ds(16, 32)], R, right),
            (edge_l, halo_r.at[pl.ds(16, 32)], R, left),
            (edge_r.at[pl.ds(16, 16)], halo_l.at[pl.ds(0, 16)], down, right),
            (edge_r.at[pl.ds(0, 16)], halo_l.at[pl.ds(48, 16)], up, right),
            (edge_l.at[pl.ds(16, 16)], halo_r.at[pl.ds(0, 16)], down, left),
            (edge_l.at[pl.ds(0, 16)], halo_r.at[pl.ds(48, 16)], up, left),
        )
        return [
            pltpu.make_async_remote_copy(
                src_ref=src, dst_ref=dst, send_sem=halo_send.at[n], recv_sem=halo_recv.at[n],
                device_id={"row": r, "col": c}, device_id_type=MESH,
            )
            for n, (src, dst, r, c) in enumerate(plan)
        ]

    halos = halo_copies()
    for copy in halos:
        copy.start()
    perms[0] = perm_image()
    perms[1] = perm_image_back()
    perms[2] = perm_swap()
    perms[3] = perm_grid()
    perms[4] = perm_grid_back()
    row_head = (lax.broadcasted_iota(jnp.int32, (256, 128), 0) // 16) % 4
    lane_head = lax.broadcasted_iota(jnp.int32, (256, 128), 1) // HEAD_DIM
    ones[...] = (row_head == lane_head).astype(F32).astype(BF)
    bias_tiles(b_bias, bias_w)
    bias_tiles(g_bias, bias_g)
    w_half[...] = w_expand[...] * jnp.asarray(0.5, BF)
    for n in range(9):
        tap = depth[n // 3, pl.ds(n % 3, 1), :].astype(F32) * 0.5
        taps[n] = jnp.broadcast_to(tap, (16, EXPANDED)).astype(BF)

    def expand(tokens, row0, row1, keep):
        x = dot(perms[0], tokens)
        if keep is not None:
            image_p[keep] = x.astype(BF)
        normed = layer_norm(x).astype(BF)
        for n in range(4):
            ch = slice(256 * n, 256 * n + 256)
            h = gelu_of_half(dot(normed, w_half[:, ch])).astype(BF)
            hidden[row0, 1:9, :, ch] = h[:128].reshape(8, 16, 256)
            hidden[row1, 1:9, :, ch] = h[128:].reshape(8, 16, 256)

    def expand_image(b):
        rows = image[pl.ds(2 * b, 2)].reshape(256, WIDTH)
        expand(rows, 2 * b + 1, 2 * b + 2, b)

    def expand_images(first, last):
        def each(b, carry):
            expand_image(b)
            return carry

        lax.fori_loop(first, last, each, 0)

    expand_images(0, 16)
    for copy in halos:
        copy.wait()

    row64 = lax.broadcasted_iota(jnp.int32, (64, WIDTH), 0)
    off_grid = ((row64 <= 15) & (R == 0)) | ((row64 >= 48) & (R == 31))
    for halo, off, hid in ((halo_l, C == 0, hid_l), (halo_r, C == 3, hid_r)):
        x = jnp.where(off_grid | off, 0.0, halo[...].astype(F32))
        hid[...] = gelu_of_half(dot(layer_norm(x).astype(BF), w_half[...]))
    row256 = lax.broadcasted_iota(jnp.int32, (256, WIDTH), 0)
    off_grid = ((row256 < 128) & (R == 0)) | ((row256 >= 128) & (R == 31))
    x = jnp.where(off_grid, 0.0, halo_tb[...].reshape(256, WIDTH).astype(F32)).astype(BF)
    expand(x, 0, 33, None)

    row_s = lax.broadcasted_iota(jnp.int32, (16, EXPANDED), 0)

    def edges(r):
        from_left = pltpu.roll(hidden[r, 8].astype(F32), 1, 0)
        hidden[r, 0] = jnp.where(row_s == 0, hid_l[pl.ds(15 + r, 1), :], from_left).astype(BF)
        from_right = pltpu.roll(hidden[r, 1].astype(F32), 15, 0)
        hidden[r, 9] = jnp.where(row_s == 15, hid_r[pl.ds(15 + r, 1), :], from_right).astype(BF)

    def all_edges(r, carry):
        edges(r)
        return carry

    lax.fori_loop(0, 34, all_edges, 0)

    def convolve(b, act):
        for row in range(2):
            for n in range(8):
                ch = slice(128 * n, 128 * n + 128)
                total = None
                for dr in range(3):
                    for dc in range(3):
                        term = hidden[2 * b + row + dr, dc : dc + 8, :, ch] * taps[3 * dr + dc, :, ch]
                        total = term if total is None else total + term
                act[128 * row : 128 * row + 128, ch] = gelu_of_half(total).reshape(128, 128)

    def project(b, n, act):
        update = dot(act[...], w_project[...])
        first = (image_p[b].astype(F32) + update).astype(BF)
        tok[:, 16 * n : 16 * n + 16, :] = dot(perms[2], first).reshape(16, 16, WIDTH)

    def exchange(src_of, dst_of, send_sem, recv_sem):
        own = pltpu.make_async_copy(src_of(mine), dst_of(mine), recv_sem)
        own.start()

        for d, to in peers():
            pltpu.make_async_remote_copy(
                src_ref=src_of(d), dst_ref=dst_of(mine), send_sem=send_sem, recv_sem=recv_sem,
                device_id=to, device_id_type=MESH,
            ).start()

    def image_part(buf, k):
        return lambda d: buf.at[8 * k + d // 4, pl.ds(2 * (d % 4), 2)]

    def grid_part(buf, k):
        return lambda d: buf.at[k, d]

    def reorder_out(perm, store):
        for n in range(4):
            block = res[:, 16 * n : 16 * n + 16, :].reshape(256, WIDTH)
            store(n, dot(perm, block).astype(BF))

    def band(k, carry):
        @pl.when(k < 4)
        def _():
            acts = (act0, act1)
            for n in range(4):
                convolve(4 * k + n, acts[n % 2])
                if n:
                    project(4 * k + n - 1, n - 1, acts[(n - 1) % 2])
            project(4 * k + 3, 3, acts[1])
            attention(tok, res, b_qkv, b_out, bias_w, ones)

            def store(n, x):
                send1[pl.ds(8 * k + 2 * n, 2)] = x.reshape(2, 8, 16, WIDTH)

            reorder_out(perms[2], store)
            exchange(image_part(send1, k), grid_part(recv1, k), send_sem1.at[k], recv_sem1.at[k])

        @pl.when(k >= 1)
        def _():
            g = k - 1
            pltpu.make_async_copy(recv1.at[g], recv1.at[g], recv_sem1.at[g]).wait()
            for n in range(4):
                x = recv1[g, 8 * n : 8 * n + 8].reshape(256, WIDTH)
                tok[:, 16 * n : 16 * n + 16, :] = dot(perms[3], x).reshape(16, 16, WIDTH)
            attention(tok, res, g_qkv, g_out, bias_g, ones)

            def store(n, x):
                send2[g, 8 * n : 8 * n + 8] = x.reshape(8, 2, 16, WIDTH)

            reorder_out(perms[4], store)
            exchange_back(g)

        return carry

    def exchange_back(g):
        own = pltpu.make_async_copy(send2.at[g, mine], image_part(recv2, g)(mine), recv_sem2.at[g])
        own.start()

        for d, to in peers():
            pltpu.make_async_remote_copy(
                src_ref=send2.at[g, d], dst_ref=image_part(recv2, g)(mine),
                send_sem=send_sem2.at[g], recv_sem=recv_sem2.at[g],
                device_id=to, device_id_type=MESH,
            ).start()

    lax.fori_loop(0, 5, band, 0)

    def finish(g, carry):
        view = recv2.at[pl.ds(8 * g, 8)]
        pltpu.make_async_copy(view, view, recv_sem2.at[g]).wait()
        for n in range(4):
            x = recv2[pl.ds(8 * g + 2 * n, 2)].reshape(256, WIDTH)
            result[pl.ds(8 * g + 2 * n, 2)] = dot(perms[1], x).astype(BF).reshape(2, 128, WIDTH)
        return carry

    lax.fori_loop(0, 4, finish, 0)

    def drain(g, carry):
        part = send2.at[g, pl.ds(0, 31)]
        pltpu.make_async_copy(part, part, send_sem1.at[g]).wait()
        pltpu.make_async_copy(part, part, send_sem2.at[g]).wait()
        return carry

    lax.fori_loop(0, 4, drain, 0)


def on_device(image, w_expand, depth, w_project, b_qkv, b_out, b_bias, g_qkv, g_out, g_bias):
    vmem = pl.BlockSpec(memory_space=pltpu.VMEM)
    dma = pltpu.SemaphoreType.DMA
    return pl.pallas_call(
        kernel,
        out_shape=jax.ShapeDtypeStruct(image.shape, BF),
        in_specs=[vmem] * 10,
        out_specs=vmem,
        scratch_shapes=[
            pltpu.VMEM((2, 128, WIDTH), BF),
            pltpu.VMEM((64, WIDTH), BF),
            pltpu.VMEM((64, WIDTH), BF),
            pltpu.VMEM((32, WIDTH), BF),
            pltpu.VMEM((32, WIDTH), BF),
            pltpu.VMEM((32, 8, 16, WIDTH), BF),
            pltpu.VMEM((4, 32, 2, 16, WIDTH), BF),
            pltpu.VMEM((4, 32, 2, 16, WIDTH), BF),
            pltpu.VMEM((32, 8, 16, WIDTH), BF),
            pltpu.VMEM((34, 10, 16, EXPANDED), BF),
            pltpu.VMEM((16, 256, WIDTH), BF),
            pltpu.VMEM((WIDTH, EXPANDED), BF),
            pltpu.VMEM((9, 16, EXPANDED), BF),
            pltpu.VMEM((64, EXPANDED), F32),
            pltpu.VMEM((64, EXPANDED), F32),
            pltpu.VMEM((256, EXPANDED), BF),
            pltpu.VMEM((256, EXPANDED), BF),
            pltpu.VMEM((16, 64, WIDTH), F32),
            pltpu.VMEM((16, 64, WIDTH), BF),
            pltpu.VMEM((5, 256, 256), BF),
            pltpu.VMEM((256, 128), BF),
            pltpu.VMEM((2, 64, 256), F32),
            pltpu.VMEM((2, 64, 256), F32),
            dma((8,)),
            dma((8,)),
            dma((4,)),
            dma((4,)),
            dma((4,)),
            dma((4,)),
        ],
        compiler_params=pltpu.CompilerParams(
            collective_id=0, has_side_effects=True, vmem_limit_bytes=56 << 20
        ),
    )(
        image, w_expand, depth, w_project, b_qkv, b_out, b_bias, g_qkv, g_out, g_bias
    )


def solution(mesh):
    in_specs = (P("row", "col", None),) + (P(),) * 9
    return jax.shard_map(
        on_device, mesh=mesh, in_specs=in_specs, out_specs=P("row", "col", None), check_vma=False
    )
```

```python
import functools

import jax
import jax.numpy as jnp
from jax import lax
from jax.experimental import pallas as pl
from jax.experimental.pallas import tpu as pltpu
from jax.sharding import PartitionSpec as P

MESH = pl.DeviceIdType.MESH
HEADS = 8
HEAD_DIM = 32
WIDTH = 256
EXPANDED = 1024
LOG2E = 1.4426950408889634
ROOT2 = 1.4142135623730951
BF = jnp.bfloat16
F32 = jnp.float32


def dot(a, b):
    return jnp.dot(a, b, preferred_element_type=F32)


def dot_nt(a, b):
    return lax.dot_general(a, b, (((1,), (1,)), ((), ())), preferred_element_type=F32)


def layer_norm(v):
    mean = jnp.mean(v, axis=-1, keepdims=True)
    cen = v - mean
    var = jnp.mean(cen * cen, axis=-1, keepdims=True)
    return cen * lax.rsqrt(var + 1e-5)


def gelu_of_half(z):
    return z + z * lax.erf(z * jnp.asarray(ROOT2, z.dtype))


def perm_image():
    out = lax.broadcasted_iota(jnp.int32, (256, 256), 0)
    src = lax.broadcasted_iota(jnp.int32, (256, 256), 1)
    want = (out & 128) | ((out & 15) << 3) | ((out >> 4) & 7)
    return (src == want).astype(F32).astype(BF)


def perm_image_back():
    out = lax.broadcasted_iota(jnp.int32, (256, 256), 0)
    src = lax.broadcasted_iota(jnp.int32, (256, 256), 1)
    want = (out & 128) | ((out & 7) << 4) | ((out >> 3) & 15)
    return (src == want).astype(F32).astype(BF)


def perm_swap():
    out = lax.broadcasted_iota(jnp.int32, (256, 256), 0)
    src = lax.broadcasted_iota(jnp.int32, (256, 256), 1)
    want = ((out & 15) << 4) | (out >> 4)
    return (src == want).astype(F32).astype(BF)


def perm_grid():
    out = lax.broadcasted_iota(jnp.int32, (256, 256), 0)
    src = lax.broadcasted_iota(jnp.int32, (256, 256), 1)
    group, pos = out >> 4, out & 15
    j0, s = group >> 3, group & 7
    want = ((pos >> 1) << 5) | (j0 << 4) | ((pos & 1) << 3) | s
    return (src == want).astype(F32).astype(BF)


def perm_grid_back():
    out = lax.broadcasted_iota(jnp.int32, (256, 256), 0)
    src = lax.broadcasted_iota(jnp.int32, (256, 256), 1)
    msg, j0, jl, s = out >> 5, (out >> 4) & 1, (out >> 3) & 1, out & 7
    want = (((j0 << 3) | s) << 4) | (msg << 1) | jl
    return (src == want).astype(F32).astype(BF)


def spread(x, masks):
    return jnp.concatenate(
        [x[16 * t : 16 * t + 16] * masks[h] for t in range(4) for h in range(4)], axis=0
    )


def bias_tiles(bias, out):
    lane = lax.broadcasted_iota(jnp.int32, (64, 128), 1)
    pad = jnp.zeros((64, 64), F32)
    for n in range(2):
        wide = [jnp.concatenate([bias[4 * n + h], pad], axis=1) * LOG2E for h in range(4)]
        for pair in range(2):
            total = jnp.zeros((64, 128), F32)
            for t in range(2):
                for h in range(4):
                    to = 64 * t + 16 * h
                    moved = pltpu.roll(wide[h], (to - 16 * (2 * pair + t)) % 128, 1)
                    total = jnp.where((lane >= to) & (lane < to + 16), moved, total)
            out[n, :, 128 * pair : 128 * pair + 128] = total


def attention(tok, res, w_qkv, w_out, bias, ones):
    lane = lax.broadcasted_iota(jnp.int32, (256, 128), 1)
    high = lane >= 64
    mlane = lax.broadcasted_iota(jnp.int32, (16, 128), 1)
    masks = [(mlane // HEAD_DIM == h).astype(F32).astype(BF) for h in range(4)]
    groups = [slice(64 * g, 64 * g + 64) for g in range(4)]
    halves = (slice(0, 128), slice(128, 256))

    def project(c):
        t = tok[pl.ds(4 * c, 4)].reshape(256, WIDTH)
        qkv = dot(layer_norm(t).astype(BF), w_qkv[...])
        q = (qkv[:, :WIDTH] * (LOG2E / HEAD_DIM**0.5)).astype(BF)
        return q, qkv[:, WIDTH : 2 * WIDTH].astype(BF), qkv[:, 2 * WIDTH :].astype(BF)

    def scores(q, k, v):
        tiles = []
        for n, half in enumerate(halves):
            z = jnp.concatenate(
                [dot_nt(q[g, half], spread(k[g, half], masks)) + bias[n] for g in groups], axis=0
            )
            tiles.append((z[:, :128], z[:, 128:]))
        return v, tiles

    def weigh(v, tiles):
        tops = [jnp.maximum(*pair) for pair in tiles]
        m = jnp.maximum(
            jnp.where(high, tops[0], tops[1]), pltpu.roll(jnp.where(high, tops[1], tops[0]), 64, 1)
        )
        for bit in (8, 4, 2, 1):
            m = jnp.maximum(m, jnp.take_along_axis(m, lane ^ bit, axis=1))
        other = pltpu.roll(m, 64, 1)
        tops = (jnp.where(high, m, other), jnp.where(high, other, m))
        return v, [
            jnp.concatenate([jnp.exp2(x - tops[n]).astype(BF) for x in tiles[n]], axis=1)
            for n in range(2)
        ]

    def mix(c, v, weights):
        mixed = []
        for n, half in enumerate(halves):
            p = weights[n]
            den = dot(p, ones[...])
            num = jnp.concatenate([dot(p[g], spread(v[g, half], masks)) for g in groups], axis=0)
            mixed.append((num / den).astype(BF))
        out = dot(jnp.concatenate(mixed, axis=1), w_out[...])
        out = out + tok[pl.ds(4 * c, 4)].reshape(256, WIDTH)
        res[pl.ds(4 * c, 4)] = out.astype(BF).reshape(4, 64, WIDTH)

    first, second, third = {}, {}, {}
    for i in range(7):
        if i < 4:
            first[i] = project(i)
        if 0 <= i - 1 < 4:
            second[i - 1] = scores(*first[i - 1])
        if 0 <= i - 2 < 4:
            third[i - 2] = weigh(*second[i - 2])
        if 0 <= i - 3 < 4:
            mix(i - 3, *third[i - 3])


def kernel(
    image, w_expand, depth, w_project, b_qkv, b_out, b_bias, g_qkv, g_out, g_bias,
    result,
    halo_tb, halo_l, halo_r, edge_l, edge_r, send1, recv1, send2, recv2,
    hidden, image_p, w_half, taps, hid_l, hid_r, act0, act1, tok, res, perms, ones, bias_w, bias_g,
    halo_send, halo_recv, send_sem1, recv_sem1, send_sem2, recv_sem2,
):
    R, C = lax.axis_index("row"), lax.axis_index("col")
    mine = (R // 4) * 4 + C

    def peers():
        out = []
        for i in (4, 3, 5, 2, 6, 1, 7, 0):
            row = (R + 4 * i) % 32
            for c in (2, 3, 1, 0):
                if i or c:
                    col = (C + c) % 4
                    out.append(((row // 4) * 4 + col, {"row": row, "col": col}))
        return out

    up, down = (R + 31) % 32, (R + 1) % 32
    left, right = (C + 3) % 4, (C + 1) % 4

    barrier = pltpu.get_barrier_semaphore()

    for _, to in peers():
        pl.semaphore_signal(barrier, inc=1, device_id=to, device_id_type=MESH)
    for r in (up, down):
        for c in (left, C, right):
            pl.semaphore_signal(barrier, inc=1, device_id={"row": r, "col": c}, device_id_type=MESH)

    row16 = lax.broadcasted_iota(jnp.int32, (32, 16, WIDTH), 1)
    edge_l[...] = jnp.sum(
        jnp.where(row16 == 0, image[:, 0:16, :].astype(F32), 0.0), axis=1
    ).astype(BF)
    edge_r[...] = jnp.sum(
        jnp.where(row16 == 15, image[:, 112:128, :].astype(F32), 0.0), axis=1
    ).astype(BF)

    pl.semaphore_wait(barrier, 37)

    def halo_copies():
        plan = (
            (image.at[31], halo_tb.at[0], down, C),
            (image.at[0], halo_tb.at[1], up, C),
            (edge_r, halo_l.at[pl.ds(16, 32)], R, right),
            (edge_l, halo_r.at[pl.ds(16, 32)], R, left),
            (edge_r.at[pl.ds(16, 16)], halo_l.at[pl.ds(0, 16)], down, right),
            (edge_r.at[pl.ds(0, 16)], halo_l.at[pl.ds(48, 16)], up, right),
            (edge_l.at[pl.ds(16, 16)], halo_r.at[pl.ds(0, 16)], down, left),
            (edge_l.at[pl.ds(0, 16)], halo_r.at[pl.ds(48, 16)], up, left),
        )
        return [
            pltpu.make_async_remote_copy(
                src_ref=src, dst_ref=dst, send_sem=halo_send.at[n], recv_sem=halo_recv.at[n],
                device_id={"row": r, "col": c}, device_id_type=MESH,
            )
            for n, (src, dst, r, c) in enumerate(plan)
        ]

    halos = halo_copies()
    for copy in halos:
        copy.start()
    perms[0] = perm_image()
    perms[1] = perm_image_back()
    perms[2] = perm_swap()
    perms[3] = perm_grid()
    perms[4] = perm_grid_back()
    row_head = (lax.broadcasted_iota(jnp.int32, (256, 128), 0) // 16) % 4
    lane_head = lax.broadcasted_iota(jnp.int32, (256, 128), 1) // HEAD_DIM
    ones[...] = (row_head == lane_head).astype(F32).astype(BF)
    bias_tiles(b_bias, bias_w)
    bias_tiles(g_bias, bias_g)
    w_half[...] = w_expand[...] * jnp.asarray(0.5, BF)
    for n in range(9):
        tap = depth[n // 3, pl.ds(n % 3, 1), :].astype(F32) * 0.5
        taps[n] = jnp.broadcast_to(tap, (16, EXPANDED)).astype(BF)

    def expand(tokens, row0, row1, keep):
        x = dot(perms[0], tokens)
        if keep is not None:
            image_p[keep] = x.astype(BF)
        normed = layer_norm(x).astype(BF)
        for n in range(4):
            ch = slice(256 * n, 256 * n + 256)
            h = gelu_of_half(dot(normed, w_half[:, ch])).astype(BF)
            hidden[row0, 1:9, :, ch] = h[:128].reshape(8, 16, 256)
            hidden[row1, 1:9, :, ch] = h[128:].reshape(8, 16, 256)

    def expand_image(b):
        rows = image[pl.ds(2 * b, 2)].reshape(256, WIDTH)
        expand(rows, 2 * b + 1, 2 * b + 2, b)

    def expand_images(first, last):
        def each(b, carry):
            expand_image(b)
            return carry

        lax.fori_loop(first, last, each, 0, unroll=4)

    expand_images(0, 16)
    for copy in halos:
        copy.wait()

    row64 = lax.broadcasted_iota(jnp.int32, (64, WIDTH), 0)
    off_grid = ((row64 <= 15) & (R == 0)) | ((row64 >= 48) & (R == 31))
    for halo, off, hid in ((halo_l, C == 0, hid_l), (halo_r, C == 3, hid_r)):
        x = jnp.where(off_grid | off, 0.0, halo[...].astype(F32))
        hid[...] = gelu_of_half(dot(layer_norm(x).astype(BF), w_half[...]))
    row256 = lax.broadcasted_iota(jnp.int32, (256, WIDTH), 0)
    off_grid = ((row256 < 128) & (R == 0)) | ((row256 >= 128) & (R == 31))
    x = jnp.where(off_grid, 0.0, halo_tb[...].reshape(256, WIDTH).astype(F32)).astype(BF)
    expand(x, 0, 33, None)

    row_s = lax.broadcasted_iota(jnp.int32, (16, EXPANDED), 0)

    def edges(r):
        from_left = pltpu.roll(hidden[r, 8].astype(F32), 1, 0)
        hidden[r, 0] = jnp.where(row_s == 0, hid_l[pl.ds(15 + r, 1), :], from_left).astype(BF)
        from_right = pltpu.roll(hidden[r, 1].astype(F32), 15, 0)
        hidden[r, 9] = jnp.where(row_s == 15, hid_r[pl.ds(15 + r, 1), :], from_right).astype(BF)

    def all_edges(r, carry):
        edges(r)
        return carry

    lax.fori_loop(0, 34, all_edges, 0)

    def convolve(b, act):
        for row in range(2):
            for n in range(8):
                ch = slice(128 * n, 128 * n + 128)
                total = None
                for dr in range(3):
                    for dc in range(3):
                        term = hidden[2 * b + row + dr, dc : dc + 8, :, ch] * taps[3 * dr + dc, :, ch]
                        total = term if total is None else total + term
                act[128 * row : 128 * row + 128, ch] = gelu_of_half(total).reshape(128, 128)

    def project(b, n, act):
        update = dot(act[...], w_project[...])
        first = (image_p[b].astype(F32) + update).astype(BF)
        tok[:, 16 * n : 16 * n + 16, :] = dot(perms[2], first).reshape(16, 16, WIDTH)

    def exchange(src_of, dst_of, send_sem, recv_sem):
        own = pltpu.make_async_copy(src_of(mine), dst_of(mine), recv_sem)
        own.start()

        for d, to in peers():
            pltpu.make_async_remote_copy(
                src_ref=src_of(d), dst_ref=dst_of(mine), send_sem=send_sem, recv_sem=recv_sem,
                device_id=to, device_id_type=MESH,
            ).start()

    def image_part(buf, k):
        return lambda d: buf.at[8 * k + d // 4, pl.ds(2 * (d % 4), 2)]

    def grid_part(buf, k):
        return lambda d: buf.at[k, d]

    def reorder_out(perm, store):
        for n in range(4):
            block = res[:, 16 * n : 16 * n + 16, :].reshape(256, WIDTH)
            store(n, dot(perm, block).astype(BF))

    def band(k, carry):
        @pl.when(k < 4)
        def _():
            acts = (act0, act1)
            for n in range(4):
                convolve(4 * k + n, acts[n % 2])
                if n:
                    project(4 * k + n - 1, n - 1, acts[(n - 1) % 2])
            project(4 * k + 3, 3, acts[1])
            attention(tok, res, b_qkv, b_out, bias_w, ones)

            def store(n, x):
                send1[pl.ds(8 * k + 2 * n, 2)] = x.reshape(2, 8, 16, WIDTH)

            reorder_out(perms[2], store)
            exchange(image_part(send1, k), grid_part(recv1, k), send_sem1.at[k], recv_sem1.at[k])

        @pl.when(k >= 1)
        def _():
            g = k - 1
            pltpu.make_async_copy(recv1.at[g], recv1.at[g], recv_sem1.at[g]).wait()
            for n in range(4):
                x = recv1[g, 8 * n : 8 * n + 8].reshape(256, WIDTH)
                tok[:, 16 * n : 16 * n + 16, :] = dot(perms[3], x).reshape(16, 16, WIDTH)
            attention(tok, res, g_qkv, g_out, bias_g, ones)

            def store(n, x):
                send2[g, 8 * n : 8 * n + 8] = x.reshape(8, 2, 16, WIDTH)

            reorder_out(perms[4], store)
            exchange_back(g)

        return carry

    def exchange_back(g):
        own = pltpu.make_async_copy(send2.at[g, mine], image_part(recv2, g)(mine), recv_sem2.at[g])
        own.start()

        for d, to in peers():
            pltpu.make_async_remote_copy(
                src_ref=send2.at[g, d], dst_ref=image_part(recv2, g)(mine),
                send_sem=send_sem2.at[g], recv_sem=recv_sem2.at[g],
                device_id=to, device_id_type=MESH,
            ).start()

    lax.fori_loop(0, 5, band, 0)

    def finish(g, carry):
        view = recv2.at[pl.ds(8 * g, 8)]
        pltpu.make_async_copy(view, view, recv_sem2.at[g]).wait()
        for n in range(4):
            x = recv2[pl.ds(8 * g + 2 * n, 2)].reshape(256, WIDTH)
            result[pl.ds(8 * g + 2 * n, 2)] = dot(perms[1], x).astype(BF).reshape(2, 128, WIDTH)
        return carry

    lax.fori_loop(0, 4, finish, 0)

    def drain(g, carry):
        part = send2.at[g, pl.ds(0, 31)]
        pltpu.make_async_copy(part, part, send_sem1.at[g]).wait()
        pltpu.make_async_copy(part, part, send_sem2.at[g]).wait()
        return carry

    lax.fori_loop(0, 4, drain, 0)


def on_device(image, w_expand, depth, w_project, b_qkv, b_out, b_bias, g_qkv, g_out, g_bias):
    vmem = pl.BlockSpec(memory_space=pltpu.VMEM)
    dma = pltpu.SemaphoreType.DMA
    return pl.pallas_call(
        kernel,
        out_shape=jax.ShapeDtypeStruct(image.shape, BF),
        in_specs=[vmem] * 10,
        out_specs=vmem,
        scratch_shapes=[
            pltpu.VMEM((2, 128, WIDTH), BF),
            pltpu.VMEM((64, WIDTH), BF),
            pltpu.VMEM((64, WIDTH), BF),
            pltpu.VMEM((32, WIDTH), BF),
            pltpu.VMEM((32, WIDTH), BF),
            pltpu.VMEM((32, 8, 16, WIDTH), BF),
            pltpu.VMEM((4, 32, 2, 16, WIDTH), BF),
            pltpu.VMEM((4, 32, 2, 16, WIDTH), BF),
            pltpu.VMEM((32, 8, 16, WIDTH), BF),
            pltpu.VMEM((34, 10, 16, EXPANDED), BF),
            pltpu.VMEM((16, 256, WIDTH), BF),
            pltpu.VMEM((WIDTH, EXPANDED), BF),
            pltpu.VMEM((9, 16, EXPANDED), BF),
            pltpu.VMEM((64, EXPANDED), F32),
            pltpu.VMEM((64, EXPANDED), F32),
            pltpu.VMEM((256, EXPANDED), BF),
            pltpu.VMEM((256, EXPANDED), BF),
            pltpu.VMEM((16, 64, WIDTH), F32),
            pltpu.VMEM((16, 64, WIDTH), BF),
            pltpu.VMEM((5, 256, 256), BF),
            pltpu.VMEM((256, 128), BF),
            pltpu.VMEM((2, 64, 256), F32),
            pltpu.VMEM((2, 64, 256), F32),
            dma((8,)),
            dma((8,)),
            dma((4,)),
            dma((4,)),
            dma((4,)),
            dma((4,)),
        ],
        compiler_params=pltpu.CompilerParams(
            collective_id=0, has_side_effects=True, vmem_limit_bytes=56 << 20
        ),
    )(
        image, w_expand, depth, w_project, b_qkv, b_out, b_bias, g_qkv, g_out, g_bias
    )


def solution(mesh):
    in_specs = (P("row", "col", None),) + (P(),) * 9
    return jax.shard_map(
        on_device, mesh=mesh, in_specs=in_specs, out_specs=P("row", "col", None), check_vma=False
    )
```
